32 devices in a mesh: seq: 8 (over z, y), dp: 4 (over x, core).
Axes of the slice: x: 2, y: 2, z: 4, core: 2. Of those that a mesh axis runs over, the one named last changes fastest.
Arguments:
- inputs: bfloat16 [4, 2048, 512], P('dp', 'seq'), may hold values from -6 to 6
- write_vecs: bfloat16 [4, 2048, 128], P('dp', 'seq'), may hold values from -6 to 6
- read_vecs: bfloat16 [4, 2048, 128], P('dp', 'seq'), may hold values from -0.5 to 0.5
- dt_code: int32 [4, 8, 2048], P('dp', None, 'seq'), may hold values from 1 to 10240
- a_rate: float32 [8], replicated, may hold values from 0.4 to 85.333333
- w_out: bfloat16 [512, 2560], replicated, may hold values from -0.125 to 0.125
- grad_out: bfloat16 [4, 2048, 2560], P('dp', 'seq'), may hold values from -0.59765625 to 0.59765625
Outputs:
- outputs: bfloat16 [4, 2048, 512], P('dp', 'seq')
- grad_inputs: bfloat16 [4, 2048, 512], P('dp', 'seq')
- grad_write: bfloat16 [4, 2048, 128], P('dp', 'seq')
- grad_read: bfloat16 [4, 2048, 128], P('dp', 'seq')
- grad_w_out: float32 [512, 2560], P('seq')
The draws below stay inside these ranges and needn't reach their ends.
All inputs are finite; a program needn't handle non-finite values.
Results may differ from the reference program's by a relative error of at most 0.0055.
Values sent between devices are 32-bit elements; how exact they have to be, the bound alone decides.
A program may use at most 128 MiB of HBM per device.

```python
import jax
import jax.numpy as jnp
from jax import lax

D_MODEL = 2560
HEAD_DIM = 64
STATE = 128
LOCAL_HEADS = 8
GROUP = 128
TOK_DEV = 256
SEQUENCE_LENGTH = 2048
BATCH_SEQUENCES = 4
CHANNELS = 512


def draw_dt_code(key, part):
    first_key, second_key, random_key_three = jax.random.split(jax.random.fold_in(key, 11), 3)
    blocks = SEQUENCE_LENGTH // TOK_DEV
    levels = jax.random.randint(first_key, (BATCH_SEQUENCES, LOCAL_HEADS, blocks, 1), 4, 13)
    random_bits = jax.random.randint(second_key, (BATCH_SEQUENCES, LOCAL_HEADS, blocks, TOK_DEV), 0, 1 << 20)
    label_values = (1 + random_bits % (2 * levels - 1)).reshape(BATCH_SEQUENCES, LOCAL_HEADS, SEQUENCE_LENGTH)
    spike_start = jax.random.randint(random_key_three, (BATCH_SEQUENCES, LOCAL_HEADS, 2, 1), 0, SEQUENCE_LENGTH)
    token_positions = jnp.arange(SEQUENCE_LENGTH, dtype=jnp.int32)[None, None, None, :]
    spike_spans = jnp.any(token_positions == spike_start, axis=2)
    return jnp.where(spike_spans, 5 * SEQUENCE_LENGTH, label_values).astype(jnp.int32)


def draw_a_rate(key, part):
    first_key, second_key, random_key_three = jax.random.split(jax.random.fold_in(key, 23), 3)
    order = jax.random.permutation(first_key, LOCAL_HEADS)
    fast_count = jax.random.randint(random_key_three, (), LOCAL_HEADS // 4, 3 * LOCAL_HEADS // 4 + 1)
    spread = jax.random.uniform(second_key, (LOCAL_HEADS,), jnp.float32)
    fast = order < fast_count
    slow_rate = 0.4 * jnp.exp(spread * jnp.log(2.5))
    fast_rate = SEQUENCE_LENGTH * jnp.exp(jnp.log(1.0 / 64.0) + spread * jnp.log(64.0 / 24.0))
    return jnp.where(fast, fast_rate, slow_rate).astype(jnp.float32)


def strengthened(array, key, source, target, blocks, factor):
    owner, partner = [(jnp.arange(array.shape[axis_at]) // (array.shape[axis_at] // blocks)).reshape([-1 if axis == axis_at else 1 for axis in range(array.ndim)]) for axis_at in (source, target)]
    chosen = jax.random.permutation(key, blocks)[partner]
    strong = (owner == chosen) | (owner == (partner + blocks // 2) % blocks)
    return jnp.where(strong, factor * array, array)


def steps_of(stream_key, dims, shards, low, top_value):
    loudness, own = 1.0, jax.random.fold_in(stream_key, 6)
    for dim, blocks in shards:
        steps = jnp.exp(jax.random.uniform(jax.random.fold_in(own, dim), (blocks,), jnp.float32, low / len(shards), top_value / len(shards)))
        loudness = loudness * jnp.repeat(steps, dims[dim] // blocks).reshape([-1 if axis == dim else 1 for axis in range(len(dims))])
    return loudness


def centred(own_key, shape, scale, bound, shards=(), kind=jnp.bfloat16):
    factor_of = steps_of(own_key, shape, shards, -0.22, 0.18) if shards else 1.0
    result = jax.random.normal(own_key, shape, jnp.float32) * scale * factor_of
    return jnp.minimum(jnp.maximum(result, -bound), bound).astype(kind)


def heavy_noise(own_key, shape, scale, most, cuts, heavy, kind=jnp.bfloat16):
    values = scale * jax.random.normal(own_key, shape, jnp.float32)
    if cuts:
        values = values * steps_of(own_key, shape, cuts, -0.22, 0.18)
    return jnp.clip(strengthened(values, jax.random.fold_in(own_key, 3), *heavy), -most, most).astype(kind)


def setup_inputs(seed: int = 0) -> dict:
    key_of = jax.random.split(jax.random.key(seed), 8)
    inputs = heavy_noise(key_of[0], (BATCH_SEQUENCES, SEQUENCE_LENGTH, CHANNELS), 1.0, 6.0, ((0, 4), (1, 8)), (1, 2, 8, 2.0))
    write_vecs = centred(key_of[1], (BATCH_SEQUENCES, SEQUENCE_LENGTH, STATE), 1.0, 6.0, ((0, 4), (1, 8)))
    read_vecs = centred(key_of[2], (BATCH_SEQUENCES, SEQUENCE_LENGTH, STATE), STATE ** -0.5, 0.5, ((0, 4), (1, 8)))
    dt_code = draw_dt_code(jax.random.fold_in(key_of[7], 71), 0)
    a_rate = draw_a_rate(jax.random.fold_in(key_of[7], 71), 0)
    w_out = centred(key_of[5], (CHANNELS, D_MODEL), D_MODEL ** -0.5, 0.125)
    grad_out = centred(key_of[6], (BATCH_SEQUENCES, SEQUENCE_LENGTH, D_MODEL), 0.1, 0.59765625, ((0, 4), (1, 8)))
    return {"inputs": inputs, "write_vecs": write_vecs, "read_vecs": read_vecs, "dt_code": dt_code, "a_rate": a_rate, "w_out": w_out, "grad_out": grad_out}


highest = lax.Precision.HIGHEST

def group_step(state, pieces):
    x_group, b_group, c_group, decay_group = pieces
    cum_decay = jnp.cumsum(decay_group, axis=1)
    rows_at = lax.broadcasted_iota(jnp.int32, (GROUP, GROUP), 0)
    cols_at = lax.broadcasted_iota(jnp.int32, (GROUP, GROUP), 1)
    lower_tri = rows_at >= cols_at
    spread = cum_decay[:, :, None] - cum_decay[:, None, :]
    decay_mask = jnp.exp(jnp.where(lower_tri[None], spread, -jnp.inf))
    scores = jnp.einsum('in,jn->ij', c_group, b_group, precision=highest)
    y_intra = jnp.einsum('hij,jhp->ihp', decay_mask * scores[None], x_group, precision=highest)
    y_inter = jnp.einsum('in,hpn->ihp', c_group, state, precision=highest) * jnp.exp(cum_decay).T[:, :, None]
    group_last = cum_decay[:, -1]
    tail_decay = jnp.exp(group_last[:, None] - cum_decay)
    fresh = jnp.einsum('jhp,jn->hpn', x_group * tail_decay.T[:, :, None], b_group, precision=highest)
    return (jnp.exp(group_last)[:, None, None] * state + fresh, y_intra + y_inter)

def sequence_forward(weighted, write_rows, read_rows, log_decay):
    blocks = SEQUENCE_LENGTH // GROUP
    pieces = (weighted.reshape(blocks, GROUP, LOCAL_HEADS, HEAD_DIM), write_rows.reshape(blocks, GROUP, STATE), read_rows.reshape(blocks, GROUP, STATE), log_decay.reshape(LOCAL_HEADS, blocks, GROUP).transpose(1, 0, 2))
    start = jnp.zeros((LOCAL_HEADS, HEAD_DIM, STATE), jnp.float32)
    final, results = lax.scan(group_step, start, pieces)
    return results.reshape(SEQUENCE_LENGTH, LOCAL_HEADS, HEAD_DIM)

def reference(inputs, write_vecs, read_vecs, dt_code, a_rate, w_out, grad_out):
    decay_rate = a_rate / (8.0 * SEQUENCE_LENGTH)
    log_decay = -(decay_rate[None, :, None] * dt_code.astype(jnp.float32))
    weight = jnp.sqrt(-jnp.expm1(2.0 * log_decay))
    gate_rows = jnp.transpose(weight, (0, 2, 1))[..., None]
    weighted = inputs.astype(jnp.float32).reshape(BATCH_SEQUENCES, SEQUENCE_LENGTH, LOCAL_HEADS, HEAD_DIM) * gate_rows
    write_rows = write_vecs.astype(jnp.float32)
    read_rows = read_vecs.astype(jnp.float32)

    def forward(weighted_in, write_in, read_in):
        return jax.vmap(sequence_forward)(weighted_in, write_in, read_in, log_decay)
    y_full, pullback = jax.vjp(forward, weighted, write_rows, read_rows)
    outputs = y_full.reshape(BATCH_SEQUENCES, SEQUENCE_LENGTH, CHANNELS).astype(jnp.bfloat16)
    flat_grad = grad_out.reshape(BATCH_SEQUENCES * SEQUENCE_LENGTH, D_MODEL)
    grad_y = jnp.dot(flat_grad, w_out.T, preferred_element_type=jnp.float32).astype(jnp.bfloat16)
    grad_w_out = jnp.dot(outputs.reshape(BATCH_SEQUENCES * SEQUENCE_LENGTH, CHANNELS).T, flat_grad, preferred_element_type=jnp.float32)
    grad_weighted, grad_write, grad_read = pullback(grad_y.astype(jnp.float32).reshape(BATCH_SEQUENCES, SEQUENCE_LENGTH, LOCAL_HEADS, HEAD_DIM))
    grad_inputs = (grad_weighted * gate_rows).reshape(BATCH_SEQUENCES, SEQUENCE_LENGTH, CHANNELS).astype(jnp.bfloat16)
    return (outputs, grad_inputs, grad_write.astype(jnp.bfloat16), grad_read.astype(jnp.bfloat16), grad_w_out)
```

```python
import functools

import jax
import jax.numpy as jnp
from jax import lax
from jax.experimental import pallas as pl
from jax.experimental.pallas import tpu as pltpu
from jax.sharding import PartitionSpec as P

HEAD_DIM = 64
STATE = 128
HEADS = 8
CHANNELS = HEADS * HEAD_DIM
MESH = pl.DeviceIdType.MESH
f32 = jnp.float32
bf16 = jnp.bfloat16


def dot(a, b, dims=((1,), (0,))):
    return lax.dot_general(a, b, (dims, ((), ())), preferred_element_type=f32)


NT = ((1,), (1,))
TN = ((0,), (0,))


def widen(cols):
    rows = cols.shape[0]
    return jnp.concatenate(
        [jnp.broadcast_to(cols[:, h : h + 1], (rows, HEAD_DIM)) for h in range(HEADS)], axis=1
    )


def one_minus_exp(w):
    series = 1.0 - w * (1.0 / 9.0)
    for k in (8, 7, 6, 5, 4, 3, 2):
        series = 1.0 - w * (1.0 / k) * series
    return jnp.where(w < 0.5, w * series, 1.0 - jnp.exp(-w))


def kernel(
    n, m, seq_len,
    x_ref, b_ref, c_ref, dt_ref, arow_ref, acol_ref, w_ref, g_ref,
    out_ref, gin_ref, gwrite_ref, gread_ref, gw_ref,
    gsend, gall, fsend, frecv, fback, fin, asend, arecv, aback, ain,
    oall, part, rsbuf, gwall,
    g_ss, g_rs, f_ss, f_rs, a_ss, a_rs, fb_ss, fb_rs, ab_ss, ab_rs,
    o_ss, o_rs, r_ss, r_rs, w_ss, w_rs,
):
    me = lax.axis_index("seq")
    dp = lax.axis_index("dp")
    tokens = x_ref.shape[1]
    rows = CHANNELS // n
    per_head = HEAD_DIM // rows
    cols = gsend.shape[2]

    def seq_copy(src, dst, ss, rs, k, wait):
        to = lax.rem(me + k, n)
        source = lax.rem(me + n - k, n)
        return pltpu.make_async_remote_copy(
            src_ref=src.at[to],
            dst_ref=dst.at[source] if wait else dst.at[me],
            send_sem=ss.at[k],
            recv_sem=rs.at[k],
            device_id={"seq": to},
            device_id_type=MESH,
        )

    def seq_start(src, dst, ss, rs):
        def body(k, carry):
            seq_copy(src, dst, ss, rs, k, False).start()
            return carry

        lax.fori_loop(1, n, body, 0)

    def seq_wait(src, dst, ss, rs):
        def body(k, carry):
            seq_copy(src, dst, ss, rs, k, True).wait()
            return carry

        lax.fori_loop(1, n, body, 0)

    def dp_copy(src, dst, ss, rs, k, wait):
        to = lax.rem(dp + k, m)
        source = lax.rem(dp + m - k, m)
        return pltpu.make_async_remote_copy(
            src_ref=src.at[to],
            dst_ref=dst.at[source] if wait else dst.at[dp],
            send_sem=ss.at[k],
            recv_sem=rs.at[k],
            device_id={"dp": to},
            device_id_type=MESH,
        )

    def dp_gather(buf, ss, rs):
        held, bit, copies = [0], m // 2, []
        while bit:
            step = []
            for off in held:
                slot = jnp.bitwise_xor(dp, off)
                copy = pltpu.make_async_remote_copy(
                    src_ref=buf.at[slot],
                    dst_ref=buf.at[slot],
                    send_sem=ss.at[off + bit],
                    recv_sem=rs.at[off + bit],
                    device_id={"dp": jnp.bitwise_xor(dp, bit)},
                    device_id_type=MESH,
                )
                copy.start()
                step.append(copy)
            for off in held:
                slot = jnp.bitwise_xor(dp, off + bit)
                pltpu.make_async_remote_copy(
                    src_ref=buf.at[slot],
                    dst_ref=buf.at[slot],
                    send_sem=ss.at[off + bit],
                    recv_sem=rs.at[off + bit],
                    device_id={"dp": jnp.bitwise_xor(dp, bit)},
                    device_id_type=MESH,
                ).wait_recv()
            copies += step
            held = held + [off + bit for off in held]
            bit //= 2
        for copy in copies:
            copy.wait_send()

    barrier = pltpu.get_barrier_semaphore()

    def greet_seq(k, carry):
        pl.semaphore_signal(
            barrier, inc=1, device_id={"seq": lax.rem(me + k, n)}, device_id_type=MESH
        )
        return carry

    def greet_dp(k, carry):
        pl.semaphore_signal(
            barrier, inc=1, device_id={"dp": lax.rem(dp + k, m)}, device_id_type=MESH
        )
        return carry

    lax.fori_loop(1, n, greet_seq, 0)
    lax.fori_loop(1, m, greet_dp, 0)

    dt = dt_ref[0]
    at_row = lax.broadcasted_iota(jnp.int32, (tokens, tokens), 0)
    at_col = lax.broadcasted_iota(jnp.int32, (tokens, tokens), 1)
    lower = at_row >= at_col
    low_mat = lower.astype(f32).astype(bf16)
    eye = (at_row == at_col).astype(f32).astype(bf16)
    digits = [
        part_of.astype(f32).astype(bf16) for part_of in (dt & 127, (dt >> 7) & 127, dt >> 14)
    ]

    def joined(pieces):
        whole = [p.astype(jnp.int32) for p in pieces]
        return whole[0] + whole[1] * 128 + whole[2] * 16384

    cum_row = joined([dot(d, low_mat, NT) for d in digits])
    cum_col = joined([dot(low_mat, d, NT) for d in digits])
    dt_col = joined([dot(eye, d, NT) for d in digits])
    rate_row = arow_ref[...] * (1.0 / (8.0 * seq_len))
    rate_col = acol_ref[...] * (1.0 / (8.0 * seq_len))
    weight = jnp.sqrt(one_minus_exp(2.0 * (rate_row * dt_col.astype(f32))))
    head = jnp.exp(-(rate_row * cum_col.astype(f32)))
    tail = jnp.exp(-(rate_row * (cum_col[tokens - 1 :, :] - cum_col).astype(f32)))
    totals = jnp.broadcast_to(
        jnp.exp(-(rate_col * cum_row[:, tokens - 1 :].astype(f32))), (HEADS, STATE)
    )
    weight_w, head_w, tail_w = widen(weight), widen(head), widen(tail)

    b = b_ref[0]
    c = c_ref[0]
    weighted = x_ref[0].astype(f32) * weight_w
    tailed = (weighted * tail_w).astype(bf16)
    weighted = weighted.astype(bf16)
    own = dot(tailed, b, TN)
    fsend[:, :rows, :] = own.reshape(n, rows, STATE)
    fsend[:, rows:, :] = jnp.broadcast_to(totals[None], (n, HEADS, STATE))

    pl.semaphore_wait(barrier, n - 1 + m - 1)
    seq_start(fsend, frecv, f_ss, f_rs)

    grad = g_ref[0]
    for d in range(m):
        gsend[d] = grad[:, d * cols : (d + 1) * cols].astype(f32)

    def g_start(k, carry):
        dp_copy(gsend, gall, g_ss, g_rs, k, False).start()
        return carry

    def g_wait(k, carry):
        dp_copy(gsend, gall, g_ss, g_rs, k, True).wait()
        return carry

    lax.fori_loop(1, m, g_start, 0)
    gall[dp] = gsend[dp]

    grad_y = dot(grad, w_ref[...], NT).astype(bf16)
    grad_dec = (grad_y.astype(f32) * head_w).astype(bf16)
    own_adj = dot(grad_dec, c, TN)
    asend[:, :rows, :] = own_adj.reshape(n, rows, STATE)
    asend[:, rows:, :] = jnp.broadcast_to(totals[None], (n, HEADS, STATE))
    seq_start(asend, arecv, a_ss, a_rs)

    my_head = (me * rows) // HEAD_DIM
    frecv[me] = fsend[me]
    arecv[me] = asend[me]

    def scan_rows(buf, back, reverse):
        def body(step, state):
            s = n - 1 - step if reverse else step
            back[s] = state
            decay = buf[s, pl.ds(rows + my_head, 1), :]
            return decay * state + buf[s, :rows, :]

        lax.fori_loop(0, n, body, jnp.zeros((rows, STATE), f32))

    seq_wait(fsend, frecv, f_ss, f_rs)
    scan_rows(frecv, fback, False)
    seq_start(fback, fin, fb_ss, fb_rs)
    fin[me] = fback[me]
    seq_wait(asend, arecv, a_ss, a_rs)
    scan_rows(arecv, aback, True)
    seq_start(aback, ain, ab_ss, ab_rs)
    ain[me] = aback[me]

    scores = dot(c, b, NT)
    pair = jnp.zeros((tokens, tokens), f32)
    y_parts, gx_parts = [], []
    for h in range(HEADS):
        span = slice(h * HEAD_DIM, (h + 1) * HEAD_DIM)
        gap = (cum_col[:, h : h + 1] - cum_row[h : h + 1, :]).astype(f32)
        mask = jnp.exp(jnp.where(lower, -(rate_row[:, h : h + 1] * gap), -jnp.inf))
        mixed = (mask * scores).astype(bf16)
        w_h, g_h = weighted[:, span], grad_y[:, span]
        y_parts.append(dot(mixed, w_h))
        gx_parts.append(dot(mixed, g_h, TN))
        pair = pair + mask * dot(g_h, w_h, NT)
    y_intra = jnp.concatenate(y_parts, axis=1)
    gx_intra = jnp.concatenate(gx_parts, axis=1)
    pair = pair.astype(bf16)
    read_intra = dot(pair, b)
    write_intra = dot(pair, c, TN)

    seq_wait(fback, fin, fb_ss, fb_rs)
    state_in = fin[...].reshape(CHANNELS, STATE).astype(bf16)
    out = (y_intra + dot(c, state_in, NT) * head_w).astype(bf16)
    out_ref[0] = out
    oall[dp] = out.astype(f32)
    dp_gather(oall, o_ss, o_rs)
    lax.fori_loop(1, m, g_wait, 0)
    total = jnp.zeros((CHANNELS, cols), f32)
    for d in range(m):
        total = total + dot(oall[d].astype(bf16), gall[d].astype(bf16), TN)
    part[...] = total.reshape(n, rows, cols)
    seq_start(part, rsbuf, r_ss, r_rs)

    gread_ref[0] = (read_intra + dot(grad_dec, state_in)).astype(bf16)
    seq_wait(aback, ain, ab_ss, ab_rs)
    adj_in = ain[...].reshape(CHANNELS, STATE).astype(bf16)
    gwrite_ref[0] = (write_intra + dot(tailed, adj_in)).astype(bf16)
    gin_ref[0] = ((gx_intra + tail_w * dot(b, adj_in, NT)) * weight_w).astype(bf16)

    def add_rows(k, acc):
        seq_copy(part, rsbuf, r_ss, r_rs, k, True).wait()
        return acc + rsbuf[lax.rem(me + n - k, n)]

    gwall[dp] = lax.fori_loop(1, n, add_rows, part[me])
    dp_gather(gwall, w_ss, w_rs)
    for d in range(m):
        gw_ref[:, d * cols : (d + 1) * cols] = gwall[d]


def solution(mesh):
    n, m = mesh.shape["seq"], mesh.shape["dp"]

    def shards(inputs, write_vecs, read_vecs, dt_code, a_rate, w_out, grad_out):
        tokens, width = inputs.shape[1], grad_out.shape[2]
        rows, cols = CHANNELS // n, width // m
        vm = pl.BlockSpec(memory_space=pltpu.VMEM)
        sems = []
        for count in (m, n, n, n, n, m, n, m):
            sems += [pltpu.SemaphoreType.DMA((count,))] * 2
        wide, plain = (n, rows + HEADS, STATE), (n, rows, STATE)
        return pl.pallas_call(
            functools.partial(kernel, n, m, float(tokens * n)),
            out_shape=(
                jax.ShapeDtypeStruct((1, tokens, CHANNELS), bf16),
                jax.ShapeDtypeStruct((1, tokens, CHANNELS), bf16),
                jax.ShapeDtypeStruct((1, tokens, STATE), bf16),
                jax.ShapeDtypeStruct((1, tokens, STATE), bf16),
                jax.ShapeDtypeStruct((rows, width), f32),
            ),
            in_specs=[vm] * 8,
            out_specs=(vm,) * 5,
            scratch_shapes=[
                pltpu.VMEM((m, tokens, cols), f32),
                pltpu.VMEM((m, tokens, cols), f32),
                pltpu.VMEM(wide, f32),
                pltpu.VMEM(wide, f32),
                pltpu.VMEM(plain, f32),
                pltpu.VMEM(plain, f32),
                pltpu.VMEM(wide, f32),
                pltpu.VMEM(wide, f32),
                pltpu.VMEM(plain, f32),
                pltpu.VMEM(plain, f32),
                pltpu.VMEM((m, tokens, CHANNELS), f32),
                pltpu.VMEM((n, rows, cols), f32),
                pltpu.VMEM((n, rows, cols), f32),
                pltpu.VMEM((m, rows, cols), f32),
            ]
            + sems,
            compiler_params=pltpu.CompilerParams(
                collective_id=0, has_side_effects=True, vmem_limit_bytes=48 * 1024 * 1024
            ),
            name="scan_core",
        )(
            inputs,
            write_vecs,
            read_vecs,
            dt_code,
            a_rate.reshape(1, HEADS),
            a_rate.reshape(HEADS, 1),
            w_out,
            grad_out,
        )

    placed = (
        P("dp", "seq", None),
        P("dp", "seq", None),
        P("dp", "seq", None),
        P("dp", None, "seq"),
        P(),
        P(),
        P("dp", "seq", None),
    )
    return jax.shard_map(
        shards,
        mesh=mesh,
        in_specs=placed,
        out_specs=(
            P("dp", "seq", None),
            P("dp", "seq", None),
            P("dp", "seq", None),
            P("dp", "seq", None),
            P("seq", None),
        ),
        check_vma=False,
    )
```

```python
import functools

import jax
import jax.numpy as jnp
from jax import lax
from jax.experimental import pallas as pl
from jax.experimental.pallas import tpu as pltpu
from jax.sharding import PartitionSpec as P

HEAD_DIM = 64
STATE = 128
HEADS = 8
CHUNKS = 4
ORDER = (0, 3, 1, 2)
VMEM_BYTES = 60 * 1024 * 1024
CHANNELS = HEADS * HEAD_DIM
MESH = pl.DeviceIdType.MESH
f32 = jnp.float32
bf16 = jnp.bfloat16


def dot(a, b, dims=((1,), (0,))):
    return lax.dot_general(a, b, (dims, ((), ())), preferred_element_type=f32)


NT = ((1,), (1,))
TN = ((0,), (0,))


def widen(cols):
    rows = cols.shape[0]
    return jnp.concatenate(
        [jnp.broadcast_to(cols[:, h : h + 1], (rows, HEAD_DIM)) for h in range(HEADS)], axis=1
    )


def one_minus_exp(w):
    series = 1.0 - w * (1.0 / 9.0)
    for k in (8, 7, 6, 5, 4, 3, 2):
        series = 1.0 - w * (1.0 / k) * series
    return jnp.where(w < 0.5, w * series, 1.0 - jnp.exp(-w))


def kernel(
    n, m, seq_len,
    x_hbm, b_hbm, c_hbm, dt_hbm, arow_ref, w_hbm, g_hbm,
    out_hbm, gin_hbm, gwrite_hbm, gread_hbm, gw_hbm,
    x_ref, b_ref, c_ref, dt_ref, w_ref, g_ref,
    out_ref, gin_ref, gwrite_ref, gread_ref, gw_ref,
    gsend, gall, fsend, frecv, fback, fin, asend, arecv, aback, ain,
    oall, part, ybuf, rsbuf, gwall,
    g_ss, g_rs, f_ss, f_rs, a_ss, a_rs, fb_ss, fb_rs, ab_ss, ab_rs,
    o_ss, o_rs, y_ss, y_rs, r_ss, r_rs, w_ss, w_rs, in_sem, out_sem,
):
    me = lax.axis_index("seq")
    dp = lax.axis_index("dp")
    tokens = x_ref.shape[1]
    pairs = n // 2
    z, y = me // 2, lax.rem(me, 2)
    loads = [
        pltpu.make_async_copy(src, dst, in_sem.at[i])
        for i, (src, dst) in enumerate(
            [(dt_hbm, dt_ref), (x_hbm, x_ref), (b_hbm, b_ref), (c_hbm, c_ref), (g_hbm, g_ref), (w_hbm, w_ref)]
        )
    ]
    for load in loads:
        load.start()
    stores = [
        pltpu.make_async_copy(src, dst, out_sem.at[i])
        for i, (src, dst) in enumerate(
            [(out_ref, out_hbm), (gin_ref, gin_hbm), (gwrite_ref, gwrite_hbm), (gread_ref, gread_hbm), (gw_ref, gw_hbm)]
        )
    ]
    rows = CHANNELS // n
    per_head = HEAD_DIM // rows
    cols = gsend.shape[2]

    def seq_copy(src, dst, ss, rs, k, wait):
        to = lax.rem(me + k, n)
        source = lax.rem(me + n - k, n)
        return pltpu.make_async_remote_copy(
            src_ref=src.at[to],
            dst_ref=dst.at[source] if wait else dst.at[me],
            send_sem=ss.at[k],
            recv_sem=rs.at[k],
            device_id={"seq": to},
            device_id_type=MESH,
        )

    def seq_start(src, dst, ss, rs):
        def body(k, carry):
            seq_copy(src, dst, ss, rs, k, False).start()
            return carry

        lax.fori_loop(1, n, body, 0)

    def seq_wait(src, dst, ss, rs):
        def body(k, carry):
            seq_copy(src, dst, ss, rs, k, True).wait()
            return carry

        lax.fori_loop(1, n, body, 0)

    def dp_copy(src, dst, ss, rs, k, wait):
        to = lax.rem(dp + k, m)
        source = lax.rem(dp + m - k, m)
        return pltpu.make_async_remote_copy(
            src_ref=src.at[to],
            dst_ref=dst.at[source] if wait else dst.at[dp],
            send_sem=ss.at[k],
            recv_sem=rs.at[k],
            device_id={"dp": to},
            device_id_type=MESH,
        )

    bits = [1 << i for i in reversed(range(m.bit_length() - 1))]

    def dp_send(buf, ss, rs, off, bit):
        slot = jnp.bitwise_xor(dp, off)
        return pltpu.make_async_remote_copy(
            src_ref=buf.at[slot],
            dst_ref=buf.at[slot],
            send_sem=ss.at[off + bit],
            recv_sem=rs.at[off + bit],
            device_id={"dp": jnp.bitwise_xor(dp, bit)},
            device_id_type=MESH,
        )

    def dp_arrived(buf, ss, rs, off):
        slot = jnp.bitwise_xor(dp, off)
        bit = off & -off
        pltpu.make_async_remote_copy(
            src_ref=buf.at[slot],
            dst_ref=buf.at[slot],
            send_sem=ss.at[off],
            recv_sem=rs.at[off],
            device_id={"dp": jnp.bitwise_xor(dp, bit)},
            device_id_type=MESH,
        ).wait_recv()

    def dp_own(buf, ss, rs):
        for bit in bits:
            dp_send(buf, ss, rs, 0, bit).start()

    def dp_rest(buf, ss, rs):
        here = set()
        for bit in bits:
            for off in range(2 * bit, m, 2 * bit):
                if off not in here:
                    dp_arrived(buf, ss, rs, off)
                    here.add(off)
                dp_send(buf, ss, rs, off, bit).start()
        for off in range(1, m):
            if off not in here:
                dp_arrived(buf, ss, rs, off)

    def dp_sent(buf, ss, rs):
        for bit in bits:
            for off in range(0, m, 2 * bit):
                dp_send(buf, ss, rs, off, bit).wait_send()

    barrier = pltpu.get_barrier_semaphore()

    def greet_seq(k, carry):
        pl.semaphore_signal(
            barrier, inc=1, device_id={"seq": lax.rem(me + k, n)}, device_id_type=MESH
        )
        return carry

    def greet_dp(k, carry):
        pl.semaphore_signal(
            barrier, inc=1, device_id={"dp": lax.rem(dp + k, m)}, device_id_type=MESH
        )
        return carry

    lax.fori_loop(1, n, greet_seq, 0)
    lax.fori_loop(1, m, greet_dp, 0)

    loads[0].wait()
    dt = dt_ref[0]
    at_row = lax.broadcasted_iota(jnp.int32, (tokens, tokens), 0)
    at_col = lax.broadcasted_iota(jnp.int32, (tokens, tokens), 1)
    lower = at_row >= at_col
    low_mat = lower.astype(f32).astype(bf16)
    eye = (at_row == at_col).astype(f32).astype(bf16)
    digits = [
        part_of.astype(f32).astype(bf16) for part_of in (dt & 127, (dt >> 7) & 127, dt >> 14)
    ]

    def joined(pieces):
        whole = [p.astype(jnp.int32) for p in pieces]
        return whole[0] + whole[1] * 128 + whole[2] * 16384

    cum_row = joined([dot(d, low_mat, NT) for d in digits])
    cum_col = joined([dot(low_mat, d, NT) for d in digits])
    dt_col = joined([dot(eye, d, NT) for d in digits])
    rate_row = arow_ref[...] * (1.0 / (8.0 * seq_len))
    same = lax.broadcasted_iota(jnp.int32, (HEADS, HEADS), 0) == lax.broadcasted_iota(
        jnp.int32, (HEADS, HEADS), 1
    )
    rate_col = jnp.sum(jnp.where(same, rate_row, 0.0), axis=1, keepdims=True)
    weight = jnp.sqrt(one_minus_exp(2.0 * (rate_row * dt_col.astype(f32))))
    head = jnp.exp(-(rate_row * cum_col.astype(f32)))
    tail = jnp.exp(-(rate_row * (cum_col[tokens - 1 :, :] - cum_col).astype(f32)))
    totals = jnp.broadcast_to(
        jnp.exp(-(rate_col * cum_row[:, tokens - 1 :].astype(f32))), (HEADS, STATE)
    )
    weight_w, head_w, tail_w = widen(weight), widen(head), widen(tail)

    for load in loads[1:4]:
        load.wait()
    b = b_ref[0]
    c = c_ref[0]
    weighted = x_ref[0].astype(f32) * weight_w
    tailed = (weighted * tail_w).astype(bf16)
    weighted = weighted.astype(bf16)
    own = dot(tailed, b, TN)
    fsend[:, :rows, :] = own.reshape(n, rows, STATE)
    fsend[:, rows:, :] = jnp.broadcast_to(totals[None], (n, HEADS, STATE))

    pl.semaphore_wait(barrier, n - 1 + m - 1)
    seq_start(fsend, frecv, f_ss, f_rs)

    loads[4].wait()
    grad = g_ref[0]
    for d in range(m):
        gsend[d] = grad[:, d * cols : (d + 1) * cols].astype(f32)

    def g_start(k, carry):
        dp_copy(gsend, gall, g_ss, g_rs, k, False).start()
        return carry

    def g_wait(k, carry):
        dp_copy(gsend, gall, g_ss, g_rs, k, True).wait()
        return carry

    lax.fori_loop(1, m, g_start, 0)
    gall[dp] = gsend[dp]

    loads[5].wait()
    grad_y = dot(grad, w_ref[...], NT).astype(bf16)
    grad_dec = (grad_y.astype(f32) * head_w).astype(bf16)
    own_adj = dot(grad_dec, c, TN)
    asend[:, :rows, :] = own_adj.reshape(n, rows, STATE)
    asend[:, rows:, :] = jnp.broadcast_to(totals[None], (n, HEADS, STATE))
    seq_start(asend, arecv, a_ss, a_rs)

    my_head = (me * rows) // HEAD_DIM
    frecv[me] = fsend[me]
    arecv[me] = asend[me]

    def scan_rows(buf, back, reverse):
        def body(step, state):
            s = n - 1 - step if reverse else step
            back[s] = state
            decay = buf[s, pl.ds(rows + my_head, 1), :]
            return decay * state + buf[s, :rows, :]

        lax.fori_loop(0, n, body, jnp.zeros((rows, STATE), f32))

    seq_wait(fsend, frecv, f_ss, f_rs)
    scan_rows(frecv, fback, False)
    seq_start(fback, fin, fb_ss, fb_rs)
    fin[me] = fback[me]
    seq_wait(asend, arecv, a_ss, a_rs)
    scan_rows(arecv, aback, True)
    seq_start(aback, ain, ab_ss, ab_rs)
    ain[me] = aback[me]

    scores = dot(c, b, NT)
    pair = jnp.zeros((tokens, tokens), f32)
    y_parts, gx_parts = [], []
    for h in range(HEADS):
        span = slice(h * HEAD_DIM, (h + 1) * HEAD_DIM)
        gap = (cum_col[:, h : h + 1] - cum_row[h : h + 1, :]).astype(f32)
        mask = jnp.exp(jnp.where(lower, -(rate_row[:, h : h + 1] * gap), -jnp.inf))
        mixed = (mask * scores).astype(bf16)
        w_h, g_h = weighted[:, span], grad_y[:, span]
        y_parts.append(dot(mixed, w_h))
        gx_parts.append(dot(mixed, g_h, TN))
        pair = pair + mask * dot(g_h, w_h, NT)
    y_intra = jnp.concatenate(y_parts, axis=1)
    gx_intra = jnp.concatenate(gx_parts, axis=1)
    pair = pair.astype(bf16)
    read_intra = dot(pair, b)
    write_intra = dot(pair, c, TN)

    seq_wait(fback, fin, fb_ss, fb_rs)
    state_in = fin[...].reshape(CHANNELS, STATE).astype(bf16)
    out = (y_intra + dot(c, state_in, NT) * head_w).astype(bf16)
    for j in ORDER:
        oall[j, dp] = out[:, j * STATE : (j + 1) * STATE].astype(f32)
        dp_own(oall.at[j], o_ss.at[j], o_rs.at[j])
    out_ref[0] = out
    stores[0].start()
    lax.fori_loop(1, m, g_wait, 0)

    def to_partner(p, wait):
        return pltpu.make_async_remote_copy(
            src_ref=part.at[2 * p + 1 - y],
            dst_ref=ybuf.at[p],
            send_sem=y_ss.at[p],
            recv_sem=y_rs.at[p],
            device_id={"seq": 2 * z + 1 - y},
            device_id_type=MESH,
        )

    def to_owner(p, source):
        return pltpu.make_async_remote_copy(
            src_ref=part.at[2 * p + y],
            dst_ref=rsbuf.at[source],
            send_sem=r_ss.at[p],
            recv_sem=r_rs.at[source],
            device_id={"seq": 2 * p + y},
            device_id_type=MESH,
        )

    per = pairs // CHUNKS

    def multiply(j):
        dp_rest(oall.at[j], o_ss.at[j], o_rs.at[j])
        total = jnp.zeros((STATE, cols), f32)
        for d in range(m):
            total = total + dot(oall[j, d].astype(bf16), gall[d].astype(bf16), TN)
        part[2 * per * j : 2 * per * (j + 1)] = total.reshape(2 * per, rows, cols)

        def body(p, carry):
            to_partner(p, False).start()
            return carry

        lax.fori_loop(per * j, per * (j + 1), body, 0)

    def join(j):
        def body(p, carry):
            to_partner(p, True).wait_recv()
            part[2 * p + y] = part[2 * p + y] + ybuf[p]

            @pl.when(p != z)
            def _():
                to_owner(p, z).start()

            return carry

        lax.fori_loop(per * j, per * (j + 1), body, 0)

    for at, j in enumerate(ORDER):
        multiply(j)
        if at:
            join(ORDER[at - 1])
    join(ORDER[-1])

    gread_ref[0] = (read_intra + dot(grad_dec, state_in)).astype(bf16)
    stores[3].start()
    seq_wait(aback, ain, ab_ss, ab_rs)
    adj_in = ain[...].reshape(CHANNELS, STATE).astype(bf16)
    gwrite_ref[0] = (write_intra + dot(tailed, adj_in)).astype(bf16)
    stores[2].start()
    gin_ref[0] = ((gx_intra + tail_w * dot(b, adj_in, NT)) * weight_w).astype(bf16)
    stores[1].start()

    def add_rows(k, acc):
        source = lax.rem(z + k, pairs)
        to_owner(source, source).wait()
        return acc + rsbuf[source]

    gwall[dp] = lax.fori_loop(1, pairs, add_rows, part[me])
    dp_own(gwall, w_ss, w_rs)
    dp_rest(gwall, w_ss, w_rs)
    for d in range(m):
        gw_ref[:, d * cols : (d + 1) * cols] = gwall[d]
    stores[4].start()

    def sent(p, carry):
        to_partner(p, True).wait_send()
        return carry

    lax.fori_loop(0, pairs, sent, 0)
    for j in ORDER:
        dp_sent(oall.at[j], o_ss.at[j], o_rs.at[j])
    dp_sent(gwall, w_ss, w_rs)
    for store in stores:
        store.wait()


def settle(*refs):
    count = len(refs) // 2
    sem = refs[-1]
    copies = [
        pltpu.make_async_copy(refs[i], refs[count + i], sem.at[i]) for i in range(count)
    ]
    for copy in copies:
        copy.start()
    for copy in copies:
        copy.wait()


def solution(mesh):
    n, m = mesh.shape["seq"], mesh.shape["dp"]

    def shards(inputs, write_vecs, read_vecs, dt_code, a_rate, w_out, grad_out):
        tokens, width = inputs.shape[1], grad_out.shape[2]
        rows, cols = CHANNELS // n, width // m
        hbm = pl.BlockSpec(memory_space=pltpu.MemorySpace.HBM)
        vm = pl.BlockSpec(memory_space=pltpu.VMEM)
        sems = []
        for shape in ((m,), (n,), (n,), (n,), (n,), (CHUNKS, m), (n // 2,), (n // 2,), (m,)):
            sems += [pltpu.SemaphoreType.DMA(shape)] * 2
        wide, plain = (n, rows + HEADS, STATE), (n, rows, STATE)
        results = (
            jax.ShapeDtypeStruct((1, tokens, CHANNELS), bf16),
            jax.ShapeDtypeStruct((1, tokens, CHANNELS), bf16),
            jax.ShapeDtypeStruct((1, tokens, STATE), bf16),
            jax.ShapeDtypeStruct((1, tokens, STATE), bf16),
            jax.ShapeDtypeStruct((rows, width), f32),
        )
        args = (inputs, write_vecs, read_vecs, dt_code, w_out, grad_out)
        held = pl.pallas_call(
            functools.partial(kernel, n, m, float(tokens * n)),
            out_shape=results,
            in_specs=[hbm] * 4 + [vm] + [hbm] * 2,
            out_specs=(hbm,) * 5,
            scratch_shapes=[pltpu.VMEM(a.shape, a.dtype) for a in args]
            + [pltpu.VMEM(a.shape, a.dtype) for a in results]
            + [
                pltpu.VMEM((m, tokens, cols), f32),
                pltpu.VMEM((m, tokens, cols), f32),
                pltpu.VMEM(wide, f32),
                pltpu.VMEM(wide, f32),
                pltpu.VMEM(plain, f32),
                pltpu.VMEM(plain, f32),
                pltpu.VMEM(wide, f32),
                pltpu.VMEM(wide, f32),
                pltpu.VMEM(plain, f32),
                pltpu.VMEM(plain, f32),
                pltpu.VMEM((CHUNKS, m, tokens, STATE), f32),
                pltpu.VMEM((n, rows, cols), f32),
                pltpu.VMEM((n // 2, rows, cols), f32),
                pltpu.VMEM((n // 2, rows, cols), f32),
                pltpu.VMEM((m, rows, cols), f32),
            ]
            + sems
            + [pltpu.SemaphoreType.DMA((6,)), pltpu.SemaphoreType.DMA((5,))],
            compiler_params=pltpu.CompilerParams(
                collective_id=0, has_side_effects=True, vmem_limit_bytes=VMEM_BYTES
            ),
            name="scan_core",
        )(inputs, write_vecs, read_vecs, dt_code, a_rate.reshape(1, HEADS), w_out, grad_out)
        return pl.pallas_call(
            settle,
            out_shape=results,
            in_specs=[hbm] * 5,
            out_specs=(hbm,) * 5,
            scratch_shapes=[pltpu.SemaphoreType.DMA((5,))],
            compiler_params=pltpu.CompilerParams(vmem_limit_bytes=VMEM_BYTES),
            name="settle",
        )(*held)

    placed = (
        P("dp", "seq", None),
        P("dp", "seq", None),
        P("dp", "seq", None),
        P("dp", None, "seq"),
        P(),
        P(),
        P("dp", "seq", None),
    )
    return jax.shard_map(
        shards,
        mesh=mesh,
        in_specs=placed,
        out_specs=(
            P("dp", "seq", None),
            P("dp", "seq", None),
            P("dp", "seq", None),
            P("dp", "seq", None),
            P("seq", None),
        ),
        check_vma=False,
    )
```

```python
import functools

import jax
import jax.numpy as jnp
from jax import lax
from jax.experimental import pallas as pl
from jax.experimental.pallas import tpu as pltpu
from jax.sharding import PartitionSpec as P

HEAD_DIM = 64
STATE = 128
HEADS = 8
CHUNKS = 4
ORDER = (0, 3, 1, 2)
VMEM_BYTES = 60 * 1024 * 1024
CHANNELS = HEADS * HEAD_DIM
MESH = pl.DeviceIdType.MESH
f32 = jnp.float32
bf16 = jnp.bfloat16


def dot(a, b, dims=((1,), (0,))):
    return lax.dot_general(a, b, (dims, ((), ())), preferred_element_type=f32)


NT = ((1,), (1,))
TN = ((0,), (0,))


def widen(cols):
    rows = cols.shape[0]
    return jnp.concatenate(
        [jnp.broadcast_to(cols[:, h : h + 1], (rows, HEAD_DIM)) for h in range(HEADS)], axis=1
    )


def one_minus_exp(w):
    series = 1.0 - w * (1.0 / 9.0)
    for k in (8, 7, 6, 5, 4, 3, 2):
        series = 1.0 - w * (1.0 / k) * series
    return jnp.where(w < 0.5, w * series, 1.0 - jnp.exp(-w))


def kernel(
    n, m, seq_len,
    x_hbm, b_hbm, c_hbm, dt_hbm, arow_ref, w_hbm, g_hbm,
    out_hbm, gin_hbm, gwrite_hbm, gread_hbm, gw_hbm,
    x_ref, b_ref, c_ref, dt_ref, w_ref, g_ref,
    out_ref, gin_ref, gwrite_ref, gread_ref, gw_ref,
    gsend, gall, fsend, frecv, fback, fin, asend, arecv, aback, ain,
    oall, part, ybuf, rsbuf, gwall,
    g_ss, g_rs, f_ss, f_rs, a_ss, a_rs, fb_ss, fb_rs, ab_ss, ab_rs,
    o_ss, o_rs, y_ss, y_rs, r_ss, r_rs, w_ss, w_rs, in_sem, out_sem,
):
    me = lax.axis_index("seq")
    dp = lax.axis_index("dp")
    tokens = x_ref.shape[1]
    pairs = n // 2
    z, y = me // 2, lax.rem(me, 2)
    loads = [
        pltpu.make_async_copy(src, dst, in_sem.at[i])
        for i, (src, dst) in enumerate(
            [(dt_hbm, dt_ref), (x_hbm, x_ref), (b_hbm, b_ref), (c_hbm, c_ref), (g_hbm, g_ref), (w_hbm, w_ref)]
        )
    ]
    for load in loads:
        load.start()
    stores = [
        pltpu.make_async_copy(src, dst, out_sem.at[i])
        for i, (src, dst) in enumerate(
            [(out_ref, out_hbm), (gin_ref, gin_hbm), (gwrite_ref, gwrite_hbm), (gread_ref, gread_hbm), (gw_ref, gw_hbm)]
        )
    ]
    rows = CHANNELS // n
    per_head = HEAD_DIM // rows
    cols = gsend.shape[2]

    def seq_copy(src, dst, ss, rs, k, wait):
        to = lax.rem(me + k, n)
        source = lax.rem(me + n - k, n)
        return pltpu.make_async_remote_copy(
            src_ref=src.at[to],
            dst_ref=dst.at[source] if wait else dst.at[me],
            send_sem=ss.at[k],
            recv_sem=rs.at[k],
            device_id={"seq": to},
            device_id_type=MESH,
        )

    def seq_start(src, dst, ss, rs):
        def body(k, carry):
            seq_copy(src, dst, ss, rs, k, False).start()
            return carry

        lax.fori_loop(1, n, body, 0)

    def seq_wait(src, dst, ss, rs):
        def body(k, carry):
            seq_copy(src, dst, ss, rs, k, True).wait()
            return carry

        lax.fori_loop(1, n, body, 0)

    def dp_copy(src, dst, ss, rs, k, wait):
        to = lax.rem(dp + k, m)
        source = lax.rem(dp + m - k, m)
        return pltpu.make_async_remote_copy(
            src_ref=src.at[to],
            dst_ref=dst.at[source] if wait else dst.at[dp],
            send_sem=ss.at[k],
            recv_sem=rs.at[k],
            device_id={"dp": to},
            device_id_type=MESH,
        )

    bits = [1 << i for i in reversed(range(m.bit_length() - 1))]

    def dp_send(buf, ss, rs, off, bit):
        slot = jnp.bitwise_xor(dp, off)
        return pltpu.make_async_remote_copy(
            src_ref=buf.at[slot],
            dst_ref=buf.at[slot],
            send_sem=ss.at[off + bit],
            recv_sem=rs.at[off + bit],
            device_id={"dp": jnp.bitwise_xor(dp, bit)},
            device_id_type=MESH,
        )

    def dp_arrived(buf, ss, rs, off):
        slot = jnp.bitwise_xor(dp, off)
        bit = off & -off
        pltpu.make_async_remote_copy(
            src_ref=buf.at[slot],
            dst_ref=buf.at[slot],
            send_sem=ss.at[off],
            recv_sem=rs.at[off],
            device_id={"dp": jnp.bitwise_xor(dp, bit)},
            device_id_type=MESH,
        ).wait_recv()

    def dp_own(buf, ss, rs):
        for bit in bits:
            dp_send(buf, ss, rs, 0, bit).start()

    def dp_rest(buf, ss, rs):
        here = set()
        for bit in bits:
            for off in range(2 * bit, m, 2 * bit):
                if off not in here:
                    dp_arrived(buf, ss, rs, off)
                    here.add(off)
                dp_send(buf, ss, rs, off, bit).start()
        for off in range(1, m):
            if off not in here:
                dp_arrived(buf, ss, rs, off)

    def dp_sent(buf, ss, rs):
        for bit in bits:
            for off in range(0, m, 2 * bit):
                dp_send(buf, ss, rs, off, bit).wait_send()

    barrier = pltpu.get_barrier_semaphore()

    def greet_seq(k, carry):
        pl.semaphore_signal(
            barrier, inc=1, device_id={"seq": lax.rem(me + k, n)}, device_id_type=MESH
        )
        return carry

    def greet_dp(k, carry):
        pl.semaphore_signal(
            barrier, inc=1, device_id={"dp": lax.rem(dp + k, m)}, device_id_type=MESH
        )
        return carry

    lax.fori_loop(1, n, greet_seq, 0)
    lax.fori_loop(1, m, greet_dp, 0)

    loads[0].wait()
    dt = dt_ref[0]
    at_row = lax.broadcasted_iota(jnp.int32, (tokens, tokens), 0)
    at_col = lax.broadcasted_iota(jnp.int32, (tokens, tokens), 1)
    lower = at_row >= at_col
    low_mat = lower.astype(f32).astype(bf16)
    eye = (at_row == at_col).astype(f32).astype(bf16)
    digits = [
        part_of.astype(f32).astype(bf16) for part_of in (dt & 127, (dt >> 7) & 127, dt >> 14)
    ]

    def joined(pieces):
        whole = [p.astype(jnp.int32) for p in pieces]
        return whole[0] + whole[1] * 128 + whole[2] * 16384

    cum_row = joined([dot(d, low_mat, NT) for d in digits])
    cum_col = joined([dot(low_mat, d, NT) for d in digits])
    dt_col = joined([dot(eye, d, NT) for d in digits])
    rate_row = arow_ref[...] * (1.0 / (8.0 * seq_len))
    same = lax.broadcasted_iota(jnp.int32, (HEADS, HEADS), 0) == lax.broadcasted_iota(
        jnp.int32, (HEADS, HEADS), 1
    )
    rate_col = jnp.sum(jnp.where(same, rate_row, 0.0), axis=1, keepdims=True)
    weight = jnp.sqrt(one_minus_exp(2.0 * (rate_row * dt_col.astype(f32))))
    head = jnp.exp(-(rate_row * cum_col.astype(f32)))
    tail = jnp.exp(-(rate_row * (cum_col[tokens - 1 :, :] - cum_col).astype(f32)))
    totals = jnp.broadcast_to(
        jnp.exp(-(rate_col * cum_row[:, tokens - 1 :].astype(f32))), (HEADS, STATE)
    )
    weight_w, head_w, tail_w = widen(weight), widen(head), widen(tail)

    for load in loads[1:4]:
        load.wait()
    b = b_ref[0]
    c = c_ref[0]
    weighted = x_ref[0].astype(f32) * weight_w
    tailed = (weighted * tail_w).astype(bf16)
    weighted = weighted.astype(bf16)
    own = dot(tailed, b, TN)
    fsend[:, :rows, :] = own.reshape(n, rows, STATE)
    fsend[:, rows:, :] = jnp.broadcast_to(totals[None], (n, HEADS, STATE))

    pl.semaphore_wait(barrier, n - 1 + m - 1)
    seq_start(fsend, frecv, f_ss, f_rs)

    loads[4].wait()
    grad = g_ref[0]
    for d in range(m):
        gsend[d] = grad[:, d * cols : (d + 1) * cols].astype(f32)

    def g_start(k, carry):
        dp_copy(gsend, gall, g_ss, g_rs, k, False).start()
        return carry

    def g_wait(k, carry):
        dp_copy(gsend, gall, g_ss, g_rs, k, True).wait()
        return carry

    lax.fori_loop(1, m, g_start, 0)
    gall[dp] = gsend[dp]

    loads[5].wait()
    grad_y = dot(grad, w_ref[...], NT).astype(bf16)
    grad_dec = (grad_y.astype(f32) * head_w).astype(bf16)
    own_adj = dot(grad_dec, c, TN)
    asend[:, :rows, :] = own_adj.reshape(n, rows, STATE)
    asend[:, rows:, :] = jnp.broadcast_to(totals[None], (n, HEADS, STATE))
    seq_start(asend, arecv, a_ss, a_rs)

    my_head = (me * rows) // HEAD_DIM
    frecv[me] = fsend[me]
    arecv[me] = asend[me]

    def scan_rows(buf, back, reverse):
        def body(step, state):
            s = n - 1 - step if reverse else step
            back[s] = state
            decay = buf[s, pl.ds(rows + my_head, 1), :]
            return decay * state + buf[s, :rows, :]

        lax.fori_loop(0, n, body, jnp.zeros((rows, STATE), f32))

    seq_wait(fsend, frecv, f_ss, f_rs)
    scan_rows(frecv, fback, False)
    seq_start(fback, fin, fb_ss, fb_rs)
    fin[me] = fback[me]

    scores = dot(c, b, NT)
    y_parts, gx_parts = [], []

    def within(heads, pair):
        for h in heads:
            span = slice(h * HEAD_DIM, (h + 1) * HEAD_DIM)
            gap = (cum_col[:, h : h + 1] - cum_row[h : h + 1, :]).astype(f32)
            mask = jnp.exp(jnp.where(lower, -(rate_row[:, h : h + 1] * gap), -jnp.inf))
            mixed = (mask * scores).astype(bf16)
            w_h, g_h = weighted[:, span], grad_y[:, span]
            y_parts.append(dot(mixed, w_h))
            gx_parts.append(dot(mixed, g_h, TN))
            pair = pair + mask * dot(g_h, w_h, NT)
        return pair

    pair = within(range(HEADS // 2), jnp.zeros((tokens, tokens), f32))
    seq_wait(asend, arecv, a_ss, a_rs)
    scan_rows(arecv, aback, True)
    seq_start(aback, ain, ab_ss, ab_rs)
    ain[me] = aback[me]
    pair = within(range(HEADS // 2, HEADS), pair)
    y_intra = jnp.concatenate(y_parts, axis=1)
    gx_intra = jnp.concatenate(gx_parts, axis=1)
    pair = pair.astype(bf16)
    read_intra = dot(pair, b)
    write_intra = dot(pair, c, TN)

    seq_wait(fback, fin, fb_ss, fb_rs)
    state_in = fin[...].reshape(CHANNELS, STATE).astype(bf16)
    out = (y_intra + dot(c, state_in, NT) * head_w).astype(bf16)
    for j in ORDER:
        oall[j, dp] = out[:, j * STATE : (j + 1) * STATE].astype(f32)
        dp_own(oall.at[j], o_ss.at[j], o_rs.at[j])
    out_ref[0] = out
    stores[0].start()
    lax.fori_loop(1, m, g_wait, 0)

    def to_partner(p, wait):
        return pltpu.make_async_remote_copy(
            src_ref=part.at[2 * p + 1 - y],
            dst_ref=ybuf.at[p],
            send_sem=y_ss.at[p],
            recv_sem=y_rs.at[p],
            device_id={"seq": 2 * z + 1 - y},
            device_id_type=MESH,
        )

    def to_owner(p, source):
        return pltpu.make_async_remote_copy(
            src_ref=part.at[2 * p + y],
            dst_ref=rsbuf.at[source],
            send_sem=r_ss.at[p],
            recv_sem=r_rs.at[source],
            device_id={"seq": 2 * p + y},
            device_id_type=MESH,
        )

    per = pairs // CHUNKS

    def multiply(j):
        dp_rest(oall.at[j], o_ss.at[j], o_rs.at[j])
        total = jnp.zeros((STATE, cols), f32)
        for d in range(m):
            total = total + dot(oall[j, d].astype(bf16), gall[d].astype(bf16), TN)
        part[2 * per * j : 2 * per * (j + 1)] = total.reshape(2 * per, rows, cols)

        def body(p, carry):
            to_partner(p, False).start()
            return carry

        lax.fori_loop(per * j, per * (j + 1), body, 0)

    def join(j):
        def body(p, carry):
            to_partner(p, True).wait_recv()
            part[2 * p + y] = part[2 * p + y] + ybuf[p]

            @pl.when(p != z)
            def _():
                to_owner(p, z).start()

            return carry

        lax.fori_loop(per * j, per * (j + 1), body, 0)

    for at, j in enumerate(ORDER):
        multiply(j)
        if at:
            join(ORDER[at - 1])
    join(ORDER[-1])

    gread_ref[0] = (read_intra + dot(grad_dec, state_in)).astype(bf16)
    stores[3].start()
    seq_wait(aback, ain, ab_ss, ab_rs)
    adj_in = ain[...].reshape(CHANNELS, STATE).astype(bf16)
    gwrite_ref[0] = (write_intra + dot(tailed, adj_in)).astype(bf16)
    stores[2].start()
    gin_ref[0] = ((gx_intra + tail_w * dot(b, adj_in, NT)) * weight_w).astype(bf16)
    stores[1].start()

    def add_rows(k, acc):
        source = lax.rem(z + k, pairs)
        to_owner(source, source).wait()
        return acc + rsbuf[source]

    gwall[dp] = lax.fori_loop(1, pairs, add_rows, part[me])
    dp_own(gwall, w_ss, w_rs)
    dp_rest(gwall, w_ss, w_rs)
    for d in range(m):
        gw_ref[:, d * cols : (d + 1) * cols] = gwall[d]
    stores[4].start()

    def sent(p, carry):
        to_partner(p, True).wait_send()
        return carry

    lax.fori_loop(0, pairs, sent, 0)
    for j in ORDER:
        dp_sent(oall.at[j], o_ss.at[j], o_rs.at[j])
    dp_sent(gwall, w_ss, w_rs)
    for store in stores:
        store.wait()


def settle(*refs):
    sources, results, held = refs[:5], refs[5:10], refs[10:15]
    in_sem, out_sem = refs[15:]
    loads = [pltpu.make_async_copy(sources[i], held[i], in_sem.at[i]) for i in range(5)]
    stores = [pltpu.make_async_copy(held[i], results[i], out_sem.at[i]) for i in range(5)]
    for load in loads:
        load.start()
    for load, store in zip(loads, stores):
        load.wait()
        store.start()
    for store in stores:
        store.wait()


def solution(mesh):
    n, m = mesh.shape["seq"], mesh.shape["dp"]

    def shards(inputs, write_vecs, read_vecs, dt_code, a_rate, w_out, grad_out):
        tokens, width = inputs.shape[1], grad_out.shape[2]
        rows, cols = CHANNELS // n, width // m
        hbm = pl.BlockSpec(memory_space=pltpu.MemorySpace.HBM)
        vm = pl.BlockSpec(memory_space=pltpu.VMEM)
        sems = []
        for shape in ((m,), (n,), (n,), (n,), (n,), (CHUNKS, m), (n // 2,), (n // 2,), (m,)):
            sems += [pltpu.SemaphoreType.DMA(shape)] * 2
        wide, plain = (n, rows + HEADS, STATE), (n, rows, STATE)
        results = (
            jax.ShapeDtypeStruct((1, tokens, CHANNELS), bf16),
            jax.ShapeDtypeStruct((1, tokens, CHANNELS), bf16),
            jax.ShapeDtypeStruct((1, tokens, STATE), bf16),
            jax.ShapeDtypeStruct((1, tokens, STATE), bf16),
            jax.ShapeDtypeStruct((rows, width), f32),
        )
        args = (inputs, write_vecs, read_vecs, dt_code, w_out, grad_out)
        held = pl.pallas_call(
            functools.partial(kernel, n, m, float(tokens * n)),
            out_shape=results,
            in_specs=[hbm] * 4 + [vm] + [hbm] * 2,
            out_specs=(hbm,) * 5,
            scratch_shapes=[pltpu.VMEM(a.shape, a.dtype) for a in args]
            + [pltpu.VMEM(a.shape, a.dtype) for a in results]
            + [
                pltpu.VMEM((m, tokens, cols), f32),
                pltpu.VMEM((m, tokens, cols), f32),
                pltpu.VMEM(wide, f32),
                pltpu.VMEM(wide, f32),
                pltpu.VMEM(plain, f32),
                pltpu.VMEM(plain, f32),
                pltpu.VMEM(wide, f32),
                pltpu.VMEM(wide, f32),
                pltpu.VMEM(plain, f32),
                pltpu.VMEM(plain, f32),
                pltpu.VMEM((CHUNKS, m, tokens, STATE), f32),
                pltpu.VMEM((n, rows, cols), f32),
                pltpu.VMEM((n // 2, rows, cols), f32),
                pltpu.VMEM((n // 2, rows, cols), f32),
                pltpu.VMEM((m, rows, cols), f32),
            ]
            + sems
            + [pltpu.SemaphoreType.DMA((6,)), pltpu.SemaphoreType.DMA((5,))],
            compiler_params=pltpu.CompilerParams(
                collective_id=0, has_side_effects=True, vmem_limit_bytes=VMEM_BYTES
            ),
            name="scan_core",
        )(inputs, write_vecs, read_vecs, dt_code, a_rate.reshape(1, HEADS), w_out, grad_out)
        return pl.pallas_call(
            settle,
            out_shape=results,
            in_specs=[hbm] * 5,
            out_specs=(hbm,) * 5,
            scratch_shapes=[pltpu.VMEM(a.shape, a.dtype) for a in results]
            + [pltpu.SemaphoreType.DMA((5,)), pltpu.SemaphoreType.DMA((5,))],
            compiler_params=pltpu.CompilerParams(vmem_limit_bytes=VMEM_BYTES),
            name="settle",
        )(*held)

    placed = (
        P("dp", "seq", None),
        P("dp", "seq", None),
        P("dp", "seq", None),
        P("dp", None, "seq"),
        P(),
        P(),
        P("dp", "seq", None),
    )
    return jax.shard_map(
        shards,
        mesh=mesh,
        in_specs=placed,
        out_specs=(
            P("dp", "seq", None),
            P("dp", "seq", None),
            P("dp", "seq", None),
            P("dp", "seq", None),
            P("seq", None),
        ),
        check_vma=False,
    )
```

```python
import functools

import jax
import jax.numpy as jnp
from jax import lax
from jax.experimental import pallas as pl
from jax.experimental.pallas import tpu as pltpu
from jax.sharding import PartitionSpec as P

HEAD_DIM = 64
STATE = 128
HEADS = 8
HALF = 256
ALONE = 384
PIECES = ((True, 0, 256), (True, 256, 256), (False, 0, 256), (False, 256, 128))
VMEM_BYTES = 60 * 1024 * 1024
CHANNELS = HEADS * HEAD_DIM
MESH = pl.DeviceIdType.MESH
f32 = jnp.float32
bf16 = jnp.bfloat16


def dot(a, b, dims=((1,), (0,))):
    return lax.dot_general(a, b, (dims, ((), ())), preferred_element_type=f32)


NT = ((1,), (1,))
TN = ((0,), (0,))


def widen(cols):
    rows = cols.shape[0]
    return jnp.concatenate(
        [jnp.broadcast_to(cols[:, h : h + 1], (rows, HEAD_DIM)) for h in range(HEADS)], axis=1
    )


def one_minus_exp(w):
    series = 1.0 - w * (1.0 / 9.0)
    for k in (8, 7, 6, 5, 4, 3, 2):
        series = 1.0 - w * (1.0 / k) * series
    return jnp.where(w < 0.5, w * series, 1.0 - jnp.exp(-w))


def kernel(
    n, m, seq_len,
    x_hbm, b_hbm, c_hbm, dt_hbm, arow_ref, w_hbm, g_hbm,
    out_hbm, gin_hbm, gwrite_hbm, gread_hbm, gw_hbm,
    x_ref, b_ref, c_ref, dt_ref, w_ref, g_ref,
    out_ref, gin_ref, gwrite_ref, gread_ref, gw_ref,
    gsend, gall, gpsend, gprecv, fsend, frecv, fback, fin, asend, arecv, aback, ain, oall,
    part0, part1, part2, part3, ybuf0, ybuf1, ybuf2, ybuf3, rsbuf0, rsbuf1, rsbuf2, rsbuf3,
    tsend, trecv, both0, both1, gwall2, gwall3,
    g_ss, g_rs, gp_ss, gp_rs, f_ss, f_rs, a_ss, a_rs, fb_ss, fb_rs, ab_ss, ab_rs,
    o_ss, o_rs, y_ss, y_rs, r_ss, r_rs, t_ss, t_rs, b_ss, b_rs, w_ss, w_rs, in_sem, out_sem,
):
    parts, ybufs = (part0, part1, part2, part3), (ybuf0, ybuf1, ybuf2, ybuf3)
    rsbufs = (rsbuf0, rsbuf1, rsbuf2, rsbuf3)
    boths, gwalls = (both0, both1), (None, None, gwall2, gwall3)
    me = lax.axis_index("seq")
    dp = lax.axis_index("dp")
    tokens = x_ref.shape[1]
    pairs = n // 2
    z, y = me // 2, lax.rem(me, 2)
    loads = [
        pltpu.make_async_copy(src, dst, in_sem.at[i])
        for i, (src, dst) in enumerate(
            [(dt_hbm, dt_ref), (x_hbm, x_ref), (b_hbm, b_ref), (c_hbm, c_ref), (g_hbm, g_ref), (w_hbm, w_ref)]
        )
    ]
    for load in loads:
        load.start()
    stores = [
        pltpu.make_async_copy(src, dst, out_sem.at[i])
        for i, (src, dst) in enumerate(
            [(out_ref, out_hbm), (gin_ref, gin_hbm), (gwrite_ref, gwrite_hbm), (gread_ref, gread_hbm), (gw_ref, gw_hbm)]
        )
    ]
    rows = CHANNELS // n
    per_head = HEAD_DIM // rows
    cols = gsend.shape[2]
    wide = gprecv.shape[1]
    base = 2 * wide
    side = lax.rem(dp, 2)

    def seq_copy(src, dst, ss, rs, k, wait):
        to = lax.rem(me + k, n)
        source = lax.rem(me + n - k, n)
        return pltpu.make_async_remote_copy(
            src_ref=src.at[to],
            dst_ref=dst.at[source] if wait else dst.at[me],
            send_sem=ss.at[k],
            recv_sem=rs.at[k],
            device_id={"seq": to},
            device_id_type=MESH,
        )

    def seq_start(src, dst, ss, rs):
        def body(k, carry):
            seq_copy(src, dst, ss, rs, k, False).start()
            return carry

        lax.fori_loop(1, n, body, 0)

    def seq_wait(src, dst, ss, rs):
        def body(k, carry):
            seq_copy(src, dst, ss, rs, k, True).wait()
            return carry

        lax.fori_loop(1, n, body, 0)

    def dp_copy(src, dst, ss, rs, k, wait):
        to = lax.rem(dp + k, m)
        source = lax.rem(dp + m - k, m)
        return pltpu.make_async_remote_copy(
            src_ref=src.at[to],
            dst_ref=dst.at[source] if wait else dst.at[dp],
            send_sem=ss.at[k],
            recv_sem=rs.at[k],
            device_id={"dp": to},
            device_id_type=MESH,
        )

    bits = [1 << i for i in reversed(range(m.bit_length() - 1))]

    def dp_send(buf, ss, rs, off, bit):
        slot = jnp.bitwise_xor(dp, off)
        return pltpu.make_async_remote_copy(
            src_ref=buf.at[slot],
            dst_ref=buf.at[slot],
            send_sem=ss.at[off + bit],
            recv_sem=rs.at[off + bit],
            device_id={"dp": jnp.bitwise_xor(dp, bit)},
            device_id_type=MESH,
        )

    def dp_arrived(buf, ss, rs, off):
        slot = jnp.bitwise_xor(dp, off)
        bit = off & -off
        pltpu.make_async_remote_copy(
            src_ref=buf.at[slot],
            dst_ref=buf.at[slot],
            send_sem=ss.at[off],
            recv_sem=rs.at[off],
            device_id={"dp": jnp.bitwise_xor(dp, bit)},
            device_id_type=MESH,
        ).wait_recv()

    def dp_own(buf, ss, rs):
        for bit in bits:
            dp_send(buf, ss, rs, 0, bit).start()

    def dp_rest(buf, ss, rs, here=()):
        here = set(here)
        for bit in bits:
            for off in range(2 * bit, m, 2 * bit):
                if off not in here:
                    dp_arrived(buf, ss, rs, off)
                    here.add(off)
                dp_send(buf, ss, rs, off, bit).start()
        for off in range(1, m):
            if off not in here:
                dp_arrived(buf, ss, rs, off)

    def dp_sent(buf, ss, rs):
        for bit in bits:
            for off in range(0, m, 2 * bit):
                dp_send(buf, ss, rs, off, bit).wait_send()

    barrier = pltpu.get_barrier_semaphore()

    def greet_seq(k, carry):
        pl.semaphore_signal(
            barrier, inc=1, device_id={"seq": lax.rem(me + k, n)}, device_id_type=MESH
        )
        return carry

    def greet_dp(k, carry):
        pl.semaphore_signal(
            barrier, inc=1, device_id={"dp": lax.rem(dp + k, m)}, device_id_type=MESH
        )
        return carry

    lax.fori_loop(1, n, greet_seq, 0)
    lax.fori_loop(1, m, greet_dp, 0)

    loads[0].wait()
    dt = dt_ref[0]
    at_row = lax.broadcasted_iota(jnp.int32, (tokens, tokens), 0)
    at_col = lax.broadcasted_iota(jnp.int32, (tokens, tokens), 1)
    lower = at_row >= at_col
    low_mat = lower.astype(f32).astype(bf16)
    eye = (at_row == at_col).astype(f32).astype(bf16)
    digits = [
        part_of.astype(f32).astype(bf16) for part_of in (dt & 127, (dt >> 7) & 127, dt >> 14)
    ]

    def joined(pieces):
        whole = [p.astype(jnp.int32) for p in pieces]
        return whole[0] + whole[1] * 128 + whole[2] * 16384

    cum_row = joined([dot(d, low_mat, NT) for d in digits])
    cum_col = joined([dot(low_mat, d, NT) for d in digits])
    dt_col = joined([dot(eye, d, NT) for d in digits])
    rate_row = arow_ref[...] * (1.0 / (8.0 * seq_len))
    same = lax.broadcasted_iota(jnp.int32, (HEADS, HEADS), 0) == lax.broadcasted_iota(
        jnp.int32, (HEADS, HEADS), 1
    )
    rate_col = jnp.sum(jnp.where(same, rate_row, 0.0), axis=1, keepdims=True)
    weight = jnp.sqrt(one_minus_exp(2.0 * (rate_row * dt_col.astype(f32))))
    head = jnp.exp(-(rate_row * cum_col.astype(f32)))
    tail = jnp.exp(-(rate_row * (cum_col[tokens - 1 :, :] - cum_col).astype(f32)))
    totals = jnp.broadcast_to(
        jnp.exp(-(rate_col * cum_row[:, tokens - 1 :].astype(f32))), (HEADS, STATE)
    )
    weight_w, head_w, tail_w = widen(weight), widen(head), widen(tail)

    for load in loads[1:4]:
        load.wait()
    b = b_ref[0]
    c = c_ref[0]
    weighted = x_ref[0].astype(f32) * weight_w
    tailed = (weighted * tail_w).astype(bf16)
    weighted = weighted.astype(bf16)
    own = dot(tailed, b, TN)
    fsend[:, :rows, :] = own.reshape(n, rows, STATE)
    fsend[:, rows:, :] = jnp.broadcast_to(totals[None], (n, HEADS, STATE))

    pl.semaphore_wait(barrier, n - 1 + m - 1)
    seq_start(fsend, frecv, f_ss, f_rs)

    loads[4].wait()
    grad = g_ref[0]
    for d in range(m):
        gsend[d] = grad[:, base + d * cols : base + (d + 1) * cols].astype(f32)
    low_cols, high_cols = grad[:, :wide].astype(f32), grad[:, wide:base].astype(f32)
    gpsend[...] = jnp.where(side == 0, high_cols, low_cols)
    gp_own = jnp.where(side == 0, low_cols, high_cols).astype(bf16)

    def pair_copy(src, dst, ss, rs):
        return pltpu.make_async_remote_copy(
            src_ref=src,
            dst_ref=dst,
            send_sem=ss,
            recv_sem=rs,
            device_id={"dp": jnp.bitwise_xor(dp, 1)},
            device_id_type=MESH,
        )

    gp_copy = pair_copy(gpsend, gprecv, gp_ss.at[0], gp_rs.at[0])

    def g_start(k, carry):
        dp_copy(gsend, gall, g_ss, g_rs, k, False).start()
        return carry

    def g_wait(k, carry):
        dp_copy(gsend, gall, g_ss, g_rs, k, True).wait()
        return carry

    lax.fori_loop(1, m, g_start, 0)
    gp_copy.start()
    gall[dp] = gsend[dp]

    loads[5].wait()
    grad_y = dot(grad, w_ref[...], NT).astype(bf16)
    grad_dec = (grad_y.astype(f32) * head_w).astype(bf16)
    own_adj = dot(grad_dec, c, TN)
    asend[:, :rows, :] = own_adj.reshape(n, rows, STATE)
    asend[:, rows:, :] = jnp.broadcast_to(totals[None], (n, HEADS, STATE))
    seq_start(asend, arecv, a_ss, a_rs)

    my_head = (me * rows) // HEAD_DIM
    frecv[me] = fsend[me]
    arecv[me] = asend[me]

    def scan_rows(buf, back, reverse):
        def body(step, state):
            s = n - 1 - step if reverse else step
            back[s] = state
            decay = buf[s, pl.ds(rows + my_head, 1), :]
            return decay * state + buf[s, :rows, :]

        lax.fori_loop(0, n, body, jnp.zeros((rows, STATE), f32))

    seq_wait(fsend, frecv, f_ss, f_rs)
    scan_rows(frecv, fback, False)
    seq_start(fback, fin, fb_ss, fb_rs)
    fin[me] = fback[me]

    scores = dot(c, b, NT)
    y_parts, gx_parts = [], []

    def within(heads, pair):
        for h in heads:
            span = slice(h * HEAD_DIM, (h + 1) * HEAD_DIM)
            gap = (cum_col[:, h : h + 1] - cum_row[h : h + 1, :]).astype(f32)
            mask = jnp.exp(jnp.where(lower, -(rate_row[:, h : h + 1] * gap), -jnp.inf))
            mixed = (mask * scores).astype(bf16)
            w_h, g_h = weighted[:, span], grad_y[:, span]
            y_parts.append(dot(mixed, w_h))
            gx_parts.append(dot(mixed, g_h, TN))
            pair = pair + mask * dot(g_h, w_h, NT)
        return pair

    pair = within(range(HEADS // 2), jnp.zeros((tokens, tokens), f32))
    seq_wait(asend, arecv, a_ss, a_rs)
    scan_rows(arecv, aback, True)
    seq_start(aback, ain, ab_ss, ab_rs)
    ain[me] = aback[me]
    pair = within(range(HEADS // 2, HEADS), pair)
    y_intra = jnp.concatenate(y_parts, axis=1)
    gx_intra = jnp.concatenate(gx_parts, axis=1)
    pair = pair.astype(bf16)
    read_intra = dot(pair, b)
    write_intra = dot(pair, c, TN)

    seq_wait(fback, fin, fb_ss, fb_rs)
    state_in = fin[...].reshape(CHANNELS, STATE).astype(bf16)
    out = (y_intra + dot(c, state_in, NT) * head_w).astype(bf16)
    halves = CHANNELS // HALF
    for j in range(halves):
        oall[j, dp] = out[:, j * HALF : (j + 1) * HALF].astype(f32)
        dp_own(oall.at[j], o_ss.at[j], o_rs.at[j])
    out_ref[0] = out
    stores[0].start()

    def to_partner(i):
        return pltpu.make_async_remote_copy(
            src_ref=parts[i].at[1 - y],
            dst_ref=ybufs[i],
            send_sem=y_ss.at[i],
            recv_sem=y_rs.at[i],
            device_id={"seq": 2 * z + 1 - y},
            device_id_type=MESH,
        )

    def to_owner(i, p, source):
        return pltpu.make_async_remote_copy(
            src_ref=parts[i].at[y, p],
            dst_ref=rsbufs[i].at[source],
            send_sem=r_ss.at[i, p],
            recv_sem=r_rs.at[i, source],
            device_id={"seq": 2 * p + y},
            device_id_type=MESH,
        )

    def send_part(i, total):
        split = total.reshape(pairs, 2, rows, total.shape[1])
        parts[i][0] = split[:, 0]
        parts[i][1] = split[:, 1]
        to_partner(i).start()

    def join(i):
        to_partner(i).wait_recv()
        parts[i][y] = parts[i][y] + ybufs[i][...]

        def body(k, carry):
            to_owner(i, lax.rem(z + k, pairs), z).start()
            return carry

        lax.fori_loop(1, pairs, body, 0)

    def owned(i):
        def body(k, acc):
            source = lax.rem(z + k, pairs)
            to_owner(i, source, source).wait()
            return acc + rsbufs[i][source]

        return lax.fori_loop(1, pairs, body, parts[i][y, z])

    gp_copy.wait()
    gp_got = gprecv[...].astype(bf16)
    mate = jnp.bitwise_xor(dp, 1)
    for j in range(halves):
        dp_arrived(oall.at[j], o_ss.at[j], o_rs.at[j], 1)
    mate_out = [oall[j, mate].astype(bf16) for j in range(halves)]
    for i, (paired, start, size) in enumerate(PIECES):
        if paired:
            at = slice(start, start + size)
            own_sum = dot(out, gp_own[:, at], TN)
            mate_sum = jnp.concatenate([dot(o, gp_got[:, at], TN) for o in mate_out], axis=0)
            send_part(i, own_sum + mate_sum)
    gread_ref[0] = (read_intra + dot(grad_dec, state_in)).astype(bf16)
    stores[3].start()
    lax.fori_loop(1, m, g_wait, 0)
    gall_half = [gall[d].astype(bf16) for d in range(m)]
    for i in range(2):
        join(i)
        dp_rest(oall.at[i], o_ss.at[i], o_rs.at[i], (1,))

    for i, (paired, start, size) in enumerate(PIECES):
        if not paired:
            at = slice(start, start + size)
            blocks = []
            for j in range(halves):
                total = jnp.zeros((HALF, size), f32)
                for d in range(m):
                    total = total + dot(oall[j, d].astype(bf16), gall_half[d][:, at], TN)
                blocks.append(total)
            send_part(i, jnp.concatenate(blocks, axis=0))

    def across(i, at):
        return pltpu.make_async_remote_copy(
            src_ref=tsend.at[i, at],
            dst_ref=trecv.at[i, at],
            send_sem=t_ss.at[i, at],
            recv_sem=t_rs.at[i, at],
            device_id={"dp": jnp.bitwise_xor(dp, bits[at])},
            device_id_type=MESH,
        )

    far = len(bits) - 1
    for i in range(2):
        tsend[i, 0] = owned(i)
        across(i, 0).start()
        join(2 + i)

    def finish_pair(i):
        for at in range(far):
            across(i, at).wait()
            total = tsend[i, at] + trecv[i, at]
            if at + 1 < far:
                tsend[i, at + 1] = total
                across(i, at + 1).start()
        boths[i][side] = total
        pair_copy(boths[i].at[side], boths[i].at[side], b_ss.at[i], b_rs.at[i]).start()

    for i in range(2):
        finish_pair(i)
    for i in (2, 3):
        gwalls[i][dp] = owned(i)
        dp_own(gwalls[i], w_ss.at[i - 2], w_rs.at[i - 2])

    seq_wait(aback, ain, ab_ss, ab_rs)
    adj_in = ain[...].reshape(CHANNELS, STATE).astype(bf16)
    gwrite_ref[0] = (write_intra + dot(tailed, adj_in)).astype(bf16)
    stores[2].start()
    gin_ref[0] = ((gx_intra + tail_w * dot(b, adj_in, NT)) * weight_w).astype(bf16)
    stores[1].start()

    for i in range(2):
        pair_copy(boths[i].at[side], boths[i].at[1 - side], b_ss.at[i], b_rs.at[i]).wait()
        start, size = PIECES[i][1:]
        for d in range(2):
            gw_ref[:, d * wide + start : d * wide + start + size] = boths[i][d]
    for i in (2, 3):
        dp_rest(gwalls[i], w_ss.at[i - 2], w_rs.at[i - 2])
        start, size = PIECES[i][1:]
        for d in range(m):
            at = base + d * cols + start
            gw_ref[:, at : at + size] = gwalls[i][d]
    stores[4].start()

    for i in range(len(PIECES)):
        to_partner(i).wait_send()
    for j in range(halves):
        dp_sent(oall.at[j], o_ss.at[j], o_rs.at[j])
    for i in range(2):
        dp_sent(gwalls[2 + i], w_ss.at[i], w_rs.at[i])
    for store in stores:
        store.wait()


def settle(*refs):
    sources, results, held = refs[:5], refs[5:10], refs[10:15]
    in_sem, out_sem = refs[15:]
    loads = [pltpu.make_async_copy(sources[i], held[i], in_sem.at[i]) for i in range(5)]
    stores = [pltpu.make_async_copy(held[i], results[i], out_sem.at[i]) for i in range(5)]
    for load in loads:
        load.start()
    for load, store in zip(loads, stores):
        load.wait()
        store.start()
    for store in stores:
        store.wait()


def solution(mesh):
    n, m = mesh.shape["seq"], mesh.shape["dp"]

    def shards(inputs, write_vecs, read_vecs, dt_code, a_rate, w_out, grad_out):
        tokens, width = inputs.shape[1], grad_out.shape[2]
        rows, cols = CHANNELS // n, ALONE
        paired_cols = (width - m * ALONE) // 2
        far = m.bit_length() - 2
        hbm = pl.BlockSpec(memory_space=pltpu.MemorySpace.HBM)
        vm = pl.BlockSpec(memory_space=pltpu.VMEM)
        sems = []
        for shape in ((m,), (1,), (n,), (n,), (n,), (n,), (2, m), (4,), (4, n // 2), (2, far), (2,), (2, m)):
            sems += [pltpu.SemaphoreType.DMA(shape)] * 2
        wide, plain = (n, rows + HEADS, STATE), (n, rows, STATE)
        results = (
            jax.ShapeDtypeStruct((1, tokens, CHANNELS), bf16),
            jax.ShapeDtypeStruct((1, tokens, CHANNELS), bf16),
            jax.ShapeDtypeStruct((1, tokens, STATE), bf16),
            jax.ShapeDtypeStruct((1, tokens, STATE), bf16),
            jax.ShapeDtypeStruct((rows, width), f32),
        )
        args = (inputs, write_vecs, read_vecs, dt_code, w_out, grad_out)
        held = pl.pallas_call(
            functools.partial(kernel, n, m, float(tokens * n)),
            out_shape=results,
            in_specs=[hbm] * 4 + [vm] + [hbm] * 2,
            out_specs=(hbm,) * 5,
            scratch_shapes=[pltpu.VMEM(a.shape, a.dtype) for a in args]
            + [pltpu.VMEM(a.shape, a.dtype) for a in results]
            + [
                pltpu.VMEM((m, tokens, cols), f32),
                pltpu.VMEM((m, tokens, cols), f32),
                pltpu.VMEM((tokens, paired_cols), f32),
                pltpu.VMEM((tokens, paired_cols), f32),
                pltpu.VMEM(wide, f32),
                pltpu.VMEM(wide, f32),
                pltpu.VMEM(plain, f32),
                pltpu.VMEM(plain, f32),
                pltpu.VMEM(wide, f32),
                pltpu.VMEM(wide, f32),
                pltpu.VMEM(plain, f32),
                pltpu.VMEM(plain, f32),
                pltpu.VMEM((2, m, tokens, HALF), f32),
            ]
            + [pltpu.VMEM((2, n // 2, rows, size), f32) for _, _, size in PIECES]
            + [pltpu.VMEM((n // 2, rows, size), f32) for _, _, size in PIECES] * 2
            + [pltpu.VMEM((2, far, rows, PIECES[0][2]), f32)] * 2
            + [pltpu.VMEM((2, rows, size), f32) for _, _, size in PIECES[:2]]
            + [pltpu.VMEM((m, rows, size), f32) for _, _, size in PIECES[2:]]
            + sems
            + [pltpu.SemaphoreType.DMA((6,)), pltpu.SemaphoreType.DMA((5,))],
            compiler_params=pltpu.CompilerParams(
                collective_id=0, has_side_effects=True, vmem_limit_bytes=VMEM_BYTES
            ),
            name="scan_core",
        )(inputs, write_vecs, read_vecs, dt_code, a_rate.reshape(1, HEADS), w_out, grad_out)
        return pl.pallas_call(
            settle,
            out_shape=results,
            in_specs=[hbm] * 5,
            out_specs=(hbm,) * 5,
            scratch_shapes=[pltpu.VMEM(a.shape, a.dtype) for a in results]
            + [pltpu.SemaphoreType.DMA((5,)), pltpu.SemaphoreType.DMA((5,))],
            compiler_params=pltpu.CompilerParams(vmem_limit_bytes=VMEM_BYTES),
            name="settle",
        )(*held)

    placed = (
        P("dp", "seq", None),
        P("dp", "seq", None),
        P("dp", "seq", None),
        P("dp", None, "seq"),
        P(),
        P(),
        P("dp", "seq", None),
    )
    return jax.shard_map(
        shards,
        mesh=mesh,
        in_specs=placed,
        out_specs=(
            P("dp", "seq", None),
            P("dp", "seq", None),
            P("dp", "seq", None),
            P("dp", "seq", None),
            P("seq", None),
        ),
        check_vma=False,
    )
```

```python
import functools

import jax
import jax.numpy as jnp
from jax import lax
from jax.experimental import pallas as pl
from jax.experimental.pallas import tpu as pltpu
from jax.sharding import PartitionSpec as P

HEAD_DIM = 64
STATE = 128
HEADS = 8
HALF = 256
ALONE = 384
PIECES = ((True, 0, 256), (True, 256, 256), (False, 0, 256), (False, 256, 128))
VMEM_BYTES = 60 * 1024 * 1024
CHANNELS = HEADS * HEAD_DIM
MESH = pl.DeviceIdType.MESH
f32 = jnp.float32
bf16 = jnp.bfloat16


def dot(a, b, dims=((1,), (0,))):
    return lax.dot_general(a, b, (dims, ((), ())), preferred_element_type=f32)


NT = ((1,), (1,))
TN = ((0,), (0,))


def widen(cols):
    rows = cols.shape[0]
    return jnp.concatenate(
        [jnp.broadcast_to(cols[:, h : h + 1], (rows, HEAD_DIM)) for h in range(HEADS)], axis=1
    )


def one_minus_exp(w):
    series = 1.0 - w * (1.0 / 9.0)
    for k in (8, 7, 6, 5, 4, 3, 2):
        series = 1.0 - w * (1.0 / k) * series
    return jnp.where(w < 0.5, w * series, 1.0 - jnp.exp(-w))


def kernel(
    n, m, seq_len,
    x_hbm, b_hbm, c_hbm, dt_hbm, arow_ref, w_hbm, g_hbm,
    out_hbm, gin_hbm, gwrite_hbm, gread_hbm, gw_hbm,
    x_ref, b_ref, c_ref, dt_ref, w_ref, g_ref,
    out_ref, gin_ref, gwrite_ref, gread_ref, gw_ref,
    gsend, gall, gpsend, gprecv, fsend, frecv, fback, fin, asend, arecv, aback, ain, oall,
    part0, part1, part2, part3, ybuf0, ybuf1, ybuf2, ybuf3, rsbuf0, rsbuf1, rsbuf2, rsbuf3,
    tsend, trecv, both0, both1, gwall2, gwall3,
    g_ss, g_rs, gp_ss, gp_rs, f_ss, f_rs, a_ss, a_rs, fb_ss, fb_rs, ab_ss, ab_rs,
    o_ss, o_rs, y_ss, y_rs, r_ss, r_rs, t_ss, t_rs, b_ss, b_rs, w_ss, w_rs, in_sem, out_sem,
):
    parts, ybufs = (part0, part1, part2, part3), (ybuf0, ybuf1, ybuf2, ybuf3)
    rsbufs = (rsbuf0, rsbuf1, rsbuf2, rsbuf3)
    boths, gwalls = (both0, both1), (None, None, gwall2, gwall3)
    me = lax.axis_index("seq")
    dp = lax.axis_index("dp")
    tokens = x_ref.shape[1]
    pairs = n // 2
    z, y = me // 2, lax.rem(me, 2)
    loads = [
        pltpu.make_async_copy(src, dst, in_sem.at[i])
        for i, (src, dst) in enumerate(
            [(dt_hbm, dt_ref), (x_hbm, x_ref), (b_hbm, b_ref), (c_hbm, c_ref), (g_hbm, g_ref), (w_hbm, w_ref)]
        )
    ]
    for load in loads:
        load.start()
    stores = [
        pltpu.make_async_copy(src, dst, out_sem.at[i])
        for i, (src, dst) in enumerate(
            [(out_ref, out_hbm), (gin_ref, gin_hbm), (gwrite_ref, gwrite_hbm), (gread_ref, gread_hbm), (gw_ref, gw_hbm)]
        )
    ]
    rows = CHANNELS // n
    per_head = HEAD_DIM // rows
    cols = gsend.shape[2]
    wide = gprecv.shape[1]
    base = 2 * wide
    side = lax.rem(dp, 2)

    def seq_copy(src, dst, ss, rs, k, wait):
        to = lax.rem(me + k, n)
        source = lax.rem(me + n - k, n)
        return pltpu.make_async_remote_copy(
            src_ref=src.at[to],
            dst_ref=dst.at[source] if wait else dst.at[me],
            send_sem=ss.at[k],
            recv_sem=rs.at[k],
            device_id={"seq": to},
            device_id_type=MESH,
        )

    def seq_start(src, dst, ss, rs):
        def body(k, carry):
            seq_copy(src, dst, ss, rs, k, False).start()
            return carry

        lax.fori_loop(1, n, body, 0)

    def seq_wait(src, dst, ss, rs):
        def body(k, carry):
            seq_copy(src, dst, ss, rs, k, True).wait()
            return carry

        lax.fori_loop(1, n, body, 0)

    def dp_copy(src, dst, ss, rs, k, wait):
        to = lax.rem(dp + k, m)
        source = lax.rem(dp + m - k, m)
        return pltpu.make_async_remote_copy(
            src_ref=src.at[to],
            dst_ref=dst.at[source] if wait else dst.at[dp],
            send_sem=ss.at[k],
            recv_sem=rs.at[k],
            device_id={"dp": to},
            device_id_type=MESH,
        )

    bits = [1 << i for i in reversed(range(m.bit_length() - 1))]

    def dp_send(buf, ss, rs, off, bit):
        slot = jnp.bitwise_xor(dp, off)
        return pltpu.make_async_remote_copy(
            src_ref=buf.at[slot],
            dst_ref=buf.at[slot],
            send_sem=ss.at[off + bit],
            recv_sem=rs.at[off + bit],
            device_id={"dp": jnp.bitwise_xor(dp, bit)},
            device_id_type=MESH,
        )

    def dp_arrived(buf, ss, rs, off):
        slot = jnp.bitwise_xor(dp, off)
        bit = off & -off
        pltpu.make_async_remote_copy(
            src_ref=buf.at[slot],
            dst_ref=buf.at[slot],
            send_sem=ss.at[off],
            recv_sem=rs.at[off],
            device_id={"dp": jnp.bitwise_xor(dp, bit)},
            device_id_type=MESH,
        ).wait_recv()

    def dp_own(buf, ss, rs):
        for bit in bits:
            dp_send(buf, ss, rs, 0, bit).start()

    def dp_rest(buf, ss, rs, here=()):
        here = set(here)
        for bit in bits:
            for off in range(2 * bit, m, 2 * bit):
                if off not in here:
                    dp_arrived(buf, ss, rs, off)
                    here.add(off)
                dp_send(buf, ss, rs, off, bit).start()
        for off in range(1, m):
            if off not in here:
                dp_arrived(buf, ss, rs, off)

    def dp_sent(buf, ss, rs):
        for bit in bits:
            for off in range(0, m, 2 * bit):
                dp_send(buf, ss, rs, off, bit).wait_send()

    barrier = pltpu.get_barrier_semaphore()

    def greet_seq(k, carry):
        pl.semaphore_signal(
            barrier, inc=1, device_id={"seq": lax.rem(me + k, n)}, device_id_type=MESH
        )
        return carry

    def greet_dp(k, carry):
        pl.semaphore_signal(
            barrier, inc=1, device_id={"dp": lax.rem(dp + k, m)}, device_id_type=MESH
        )
        return carry

    lax.fori_loop(1, n, greet_seq, 0)
    lax.fori_loop(1, m, greet_dp, 0)

    loads[0].wait()
    dt = dt_ref[0]
    at_row = lax.broadcasted_iota(jnp.int32, (tokens, tokens), 0)
    at_col = lax.broadcasted_iota(jnp.int32, (tokens, tokens), 1)
    lower = at_row >= at_col
    low_mat = lower.astype(f32).astype(bf16)
    eye = (at_row == at_col).astype(f32).astype(bf16)
    digits = [
        part_of.astype(f32).astype(bf16) for part_of in (dt & 127, (dt >> 7) & 127, dt >> 14)
    ]

    def joined(pieces):
        whole = [p.astype(jnp.int32) for p in pieces]
        return whole[0] + whole[1] * 128 + whole[2] * 16384

    cum_row = joined([dot(d, low_mat, NT) for d in digits])
    cum_col = joined([dot(low_mat, d, NT) for d in digits])
    dt_col = joined([dot(eye, d, NT) for d in digits])
    rate_row = arow_ref[...] * (1.0 / (8.0 * seq_len))
    same = lax.broadcasted_iota(jnp.int32, (HEADS, HEADS), 0) == lax.broadcasted_iota(
        jnp.int32, (HEADS, HEADS), 1
    )
    rate_col = jnp.sum(jnp.where(same, rate_row, 0.0), axis=1, keepdims=True)
    weight = jnp.sqrt(one_minus_exp(2.0 * (rate_row * dt_col.astype(f32))))
    head = jnp.exp(-(rate_row * cum_col.astype(f32)))
    tail = jnp.exp(-(rate_row * (cum_col[tokens - 1 :, :] - cum_col).astype(f32)))
    totals = jnp.broadcast_to(
        jnp.exp(-(rate_col * cum_row[:, tokens - 1 :].astype(f32))), (HEADS, STATE)
    )
    weight_w, head_w, tail_w = widen(weight), widen(head), widen(tail)

    for load in loads[1:4]:
        load.wait()
    b = b_ref[0]
    c = c_ref[0]
    weighted = x_ref[0].astype(f32) * weight_w
    tailed = (weighted * tail_w).astype(bf16)
    weighted = weighted.astype(bf16)
    own = dot(tailed, b, TN)
    fsend[:, :rows, :] = own.reshape(n, rows, STATE)
    fsend[:, rows:, :] = jnp.broadcast_to(totals[None], (n, HEADS, STATE))

    pl.semaphore_wait(barrier, n - 1 + m - 1)
    seq_start(fsend, frecv, f_ss, f_rs)

    loads[4].wait()
    grad = g_ref[0]
    for d in range(m):
        gsend[d] = grad[:, base + d * cols : base + (d + 1) * cols].astype(f32)
    low_cols, high_cols = grad[:, :wide].astype(f32), grad[:, wide:base].astype(f32)
    gpsend[...] = jnp.where(side == 0, high_cols, low_cols)
    gp_own = jnp.where(side == 0, low_cols, high_cols).astype(bf16)

    def pair_copy(src, dst, ss, rs):
        return pltpu.make_async_remote_copy(
            src_ref=src,
            dst_ref=dst,
            send_sem=ss,
            recv_sem=rs,
            device_id={"dp": jnp.bitwise_xor(dp, 1)},
            device_id_type=MESH,
        )

    gp_copy = pair_copy(gpsend, gprecv, gp_ss.at[0], gp_rs.at[0])

    def g_start(k, carry):
        dp_copy(gsend, gall, g_ss, g_rs, k, False).start()
        return carry

    def g_wait(k, carry):
        dp_copy(gsend, gall, g_ss, g_rs, k, True).wait()
        return carry

    lax.fori_loop(1, m, g_start, 0)
    gp_copy.start()
    gall[dp] = gsend[dp]

    loads[5].wait()
    grad_y = dot(grad, w_ref[...], NT).astype(bf16)
    grad_dec = (grad_y.astype(f32) * head_w).astype(bf16)
    my_head = (me * rows) // HEAD_DIM
    frecv[me] = fsend[me]

    def scan_rows(buf, back, reverse):
        def body(step, state):
            s = n - 1 - step if reverse else step
            back[s] = state
            decay = buf[s, pl.ds(rows + my_head, 1), :]
            return decay * state + buf[s, :rows, :]

        lax.fori_loop(0, n, body, jnp.zeros((rows, STATE), f32))

    scores = dot(c, b, NT)
    y_parts, gx_parts = [], []

    def within(heads, pair):
        for h in heads:
            span = slice(h * HEAD_DIM, (h + 1) * HEAD_DIM)
            gap = (cum_col[:, h : h + 1] - cum_row[h : h + 1, :]).astype(f32)
            mask = jnp.exp(jnp.where(lower, -(rate_row[:, h : h + 1] * gap), -jnp.inf))
            mixed = (mask * scores).astype(bf16)
            w_h, g_h = weighted[:, span], grad_y[:, span]
            y_parts.append(dot(mixed, w_h))
            gx_parts.append(dot(mixed, g_h, TN))
            pair = pair + mask * dot(g_h, w_h, NT)
        return pair

    pair = within(range(HEADS // 2), jnp.zeros((tokens, tokens), f32))
    seq_wait(fsend, frecv, f_ss, f_rs)
    scan_rows(frecv, fback, False)
    seq_start(fback, fin, fb_ss, fb_rs)
    fin[me] = fback[me]

    own_adj = dot(grad_dec, c, TN)
    asend[:, :rows, :] = own_adj.reshape(n, rows, STATE)
    asend[:, rows:, :] = jnp.broadcast_to(totals[None], (n, HEADS, STATE))
    seq_start(asend, arecv, a_ss, a_rs)
    arecv[me] = asend[me]
    pair = within(range(HEADS // 2, HEADS), pair)
    y_intra = jnp.concatenate(y_parts, axis=1)
    gx_intra = jnp.concatenate(gx_parts, axis=1)
    pair = pair.astype(bf16)
    read_intra = dot(pair, b)
    write_intra = dot(pair, c, TN)

    seq_wait(fback, fin, fb_ss, fb_rs)
    state_in = fin[...].reshape(CHANNELS, STATE).astype(bf16)
    out = (y_intra + dot(c, state_in, NT) * head_w).astype(bf16)
    halves = CHANNELS // HALF
    for j in range(halves):
        oall[j, dp] = out[:, j * HALF : (j + 1) * HALF].astype(f32)
        dp_own(oall.at[j], o_ss.at[j], o_rs.at[j])
    out_ref[0] = out
    stores[0].start()

    def to_partner(i):
        return pltpu.make_async_remote_copy(
            src_ref=parts[i].at[1 - y],
            dst_ref=ybufs[i],
            send_sem=y_ss.at[i],
            recv_sem=y_rs.at[i],
            device_id={"seq": 2 * z + 1 - y},
            device_id_type=MESH,
        )

    def to_owner(i, p, source):
        return pltpu.make_async_remote_copy(
            src_ref=parts[i].at[y, p],
            dst_ref=rsbufs[i].at[source],
            send_sem=r_ss.at[i, p],
            recv_sem=r_rs.at[i, source],
            device_id={"seq": 2 * p + y},
            device_id_type=MESH,
        )

    def send_part(i, total):
        split = total.reshape(pairs, 2, rows, total.shape[1])
        parts[i][0] = split[:, 0]
        parts[i][1] = split[:, 1]
        to_partner(i).start()

    def join(i):
        to_partner(i).wait_recv()
        parts[i][y] = parts[i][y] + ybufs[i][...]

        def body(k, carry):
            to_owner(i, lax.rem(z + k, pairs), z).start()
            return carry

        lax.fori_loop(1, pairs, body, 0)

    def owned(i):
        def body(k, acc):
            source = lax.rem(z + k, pairs)
            to_owner(i, source, source).wait()
            return acc + rsbufs[i][source]

        return lax.fori_loop(1, pairs, body, parts[i][y, z])

    gp_copy.wait()
    gp_got = gprecv[...].astype(bf16)
    mate = jnp.bitwise_xor(dp, 1)
    for j in range(halves):
        dp_arrived(oall.at[j], o_ss.at[j], o_rs.at[j], 1)
    mate_out = [oall[j, mate].astype(bf16) for j in range(halves)]
    for i, (paired, start, size) in enumerate(PIECES):
        if paired:
            at = slice(start, start + size)
            own_sum = dot(out, gp_own[:, at], TN)
            mate_sum = jnp.concatenate([dot(o, gp_got[:, at], TN) for o in mate_out], axis=0)
            send_part(i, own_sum + mate_sum)
    gread_ref[0] = (read_intra + dot(grad_dec, state_in)).astype(bf16)
    stores[3].start()
    seq_wait(asend, arecv, a_ss, a_rs)
    scan_rows(arecv, aback, True)
    seq_start(aback, ain, ab_ss, ab_rs)
    ain[me] = aback[me]
    lax.fori_loop(1, m, g_wait, 0)
    gall_half = [gall[d].astype(bf16) for d in range(m)]
    for i in range(2):
        join(i)
        dp_rest(oall.at[i], o_ss.at[i], o_rs.at[i], (1,))

    for i, (paired, start, size) in enumerate(PIECES):
        if not paired:
            at = slice(start, start + size)
            blocks = []
            for j in range(halves):
                total = jnp.zeros((HALF, size), f32)
                for d in range(m):
                    total = total + dot(oall[j, d].astype(bf16), gall_half[d][:, at], TN)
                blocks.append(total)
            send_part(i, jnp.concatenate(blocks, axis=0))

    def across(i, at):
        return pltpu.make_async_remote_copy(
            src_ref=tsend.at[i, at],
            dst_ref=trecv.at[i, at],
            send_sem=t_ss.at[i, at],
            recv_sem=t_rs.at[i, at],
            device_id={"dp": jnp.bitwise_xor(dp, bits[at])},
            device_id_type=MESH,
        )

    far = len(bits) - 1
    for i in range(2):
        tsend[i, 0] = owned(i)
        across(i, 0).start()
        join(2 + i)

    def finish_pair(i):
        for at in range(far):
            across(i, at).wait()
            total = tsend[i, at] + trecv[i, at]
            if at + 1 < far:
                tsend[i, at + 1] = total
                across(i, at + 1).start()
        boths[i][side] = total
        pair_copy(boths[i].at[side], boths[i].at[side], b_ss.at[i], b_rs.at[i]).start()

    for i in range(2):
        finish_pair(i)
    for i in (2, 3):
        gwalls[i][dp] = owned(i)
        dp_own(gwalls[i], w_ss.at[i - 2], w_rs.at[i - 2])

    seq_wait(aback, ain, ab_ss, ab_rs)
    adj_in = ain[...].reshape(CHANNELS, STATE).astype(bf16)
    gwrite_ref[0] = (write_intra + dot(tailed, adj_in)).astype(bf16)
    stores[2].start()
    gin_ref[0] = ((gx_intra + tail_w * dot(b, adj_in, NT)) * weight_w).astype(bf16)
    stores[1].start()

    for i in range(2):
        pair_copy(boths[i].at[side], boths[i].at[1 - side], b_ss.at[i], b_rs.at[i]).wait()
        start, size = PIECES[i][1:]
        for d in range(2):
            gw_ref[:, d * wide + start : d * wide + start + size] = boths[i][d]
    for i in (2, 3):
        dp_rest(gwalls[i], w_ss.at[i - 2], w_rs.at[i - 2])
        start, size = PIECES[i][1:]
        for d in range(m):
            at = base + d * cols + start
            gw_ref[:, at : at + size] = gwalls[i][d]
    stores[4].start()

    for i in range(len(PIECES)):
        to_partner(i).wait_send()
    for j in range(halves):
        dp_sent(oall.at[j], o_ss.at[j], o_rs.at[j])
    for i in range(2):
        dp_sent(gwalls[2 + i], w_ss.at[i], w_rs.at[i])
    for store in stores:
        store.wait()


def settle(*refs):
    sources, results, held = refs[:5], refs[5:10], refs[10:15]
    in_sem, out_sem = refs[15:]
    loads = [pltpu.make_async_copy(sources[i], held[i], in_sem.at[i]) for i in range(5)]
    stores = [pltpu.make_async_copy(held[i], results[i], out_sem.at[i]) for i in range(5)]
    for load in loads:
        load.start()
    for load, store in zip(loads, stores):
        load.wait()
        store.start()
    for store in stores:
        store.wait()


def solution(mesh):
    n, m = mesh.shape["seq"], mesh.shape["dp"]

    def shards(inputs, write_vecs, read_vecs, dt_code, a_rate, w_out, grad_out):
        tokens, width = inputs.shape[1], grad_out.shape[2]
        rows, cols = CHANNELS // n, ALONE
        paired_cols = (width - m * ALONE) // 2
        far = m.bit_length() - 2
        hbm = pl.BlockSpec(memory_space=pltpu.MemorySpace.HBM)
        vm = pl.BlockSpec(memory_space=pltpu.VMEM)
        sems = []
        for shape in ((m,), (1,), (n,), (n,), (n,), (n,), (2, m), (4,), (4, n // 2), (2, far), (2,), (2, m)):
            sems += [pltpu.SemaphoreType.DMA(shape)] * 2
        wide, plain = (n, rows + HEADS, STATE), (n, rows, STATE)
        results = (
            jax.ShapeDtypeStruct((1, tokens, CHANNELS), bf16),
            jax.ShapeDtypeStruct((1, tokens, CHANNELS), bf16),
            jax.ShapeDtypeStruct((1, tokens, STATE), bf16),
            jax.ShapeDtypeStruct((1, tokens, STATE), bf16),
            jax.ShapeDtypeStruct((rows, width), f32),
        )
        args = (inputs, write_vecs, read_vecs, dt_code, w_out, grad_out)
        held = pl.pallas_call(
            functools.partial(kernel, n, m, float(tokens * n)),
            out_shape=results,
            in_specs=[hbm] * 4 + [vm] + [hbm] * 2,
            out_specs=(hbm,) * 5,
            scratch_shapes=[pltpu.VMEM(a.shape, a.dtype) for a in args]
            + [pltpu.VMEM(a.shape, a.dtype) for a in results]
            + [
                pltpu.VMEM((m, tokens, cols), f32),
                pltpu.VMEM((m, tokens, cols), f32),
                pltpu.VMEM((tokens, paired_cols), f32),
                pltpu.VMEM((tokens, paired_cols), f32),
                pltpu.VMEM(wide, f32),
                pltpu.VMEM(wide, f32),
                pltpu.VMEM(plain, f32),
                pltpu.VMEM(plain, f32),
                pltpu.VMEM(wide, f32),
                pltpu.VMEM(wide, f32),
                pltpu.VMEM(plain, f32),
                pltpu.VMEM(plain, f32),
                pltpu.VMEM((2, m, tokens, HALF), f32),
            ]
            + [pltpu.VMEM((2, n // 2, rows, size), f32) for _, _, size in PIECES]
            + [pltpu.VMEM((n // 2, rows, size), f32) for _, _, size in PIECES] * 2
            + [pltpu.VMEM((2, far, rows, PIECES[0][2]), f32)] * 2
            + [pltpu.VMEM((2, rows, size), f32) for _, _, size in PIECES[:2]]
            + [pltpu.VMEM((m, rows, size), f32) for _, _, size in PIECES[2:]]
            + sems
            + [pltpu.SemaphoreType.DMA((6,)), pltpu.SemaphoreType.DMA((5,))],
            compiler_params=pltpu.CompilerParams(
                collective_id=0, has_side_effects=True, vmem_limit_bytes=VMEM_BYTES
            ),
            name="scan_core",
        )(inputs, write_vecs, read_vecs, dt_code, a_rate.reshape(1, HEADS), w_out, grad_out)
        return pl.pallas_call(
            settle,
            out_shape=results,
            in_specs=[hbm] * 5,
            out_specs=(hbm,) * 5,
            scratch_shapes=[pltpu.VMEM(a.shape, a.dtype) for a in results]
            + [pltpu.SemaphoreType.DMA((5,)), pltpu.SemaphoreType.DMA((5,))],
            compiler_params=pltpu.CompilerParams(vmem_limit_bytes=VMEM_BYTES),
            name="settle",
        )(*held)

    placed = (
        P("dp", "seq", None),
        P("dp", "seq", None),
        P("dp", "seq", None),
        P("dp", None, "seq"),
        P(),
        P(),
        P("dp", "seq", None),
    )
    return jax.shard_map(
        shards,
        mesh=mesh,
        in_specs=placed,
        out_specs=(
            P("dp", "seq", None),
            P("dp", "seq", None),
            P("dp", "seq", None),
            P("dp", "seq", None),
            P("seq", None),
        ),
        check_vma=False,
    )
```

```python
import functools

import jax
import jax.numpy as jnp
from jax import lax
from jax.experimental import pallas as pl
from jax.experimental.pallas import tpu as pltpu
from jax.sharding import PartitionSpec as P

HEAD_DIM = 64
STATE = 128
HEADS = 8
HALF = 256
ALONE = 384
PIECES = ((True, 0, 256), (True, 256, 256), (False, 0, 256), (False, 256, 128))
VMEM_BYTES = 60 * 1024 * 1024
CHANNELS = HEADS * HEAD_DIM
MESH = pl.DeviceIdType.MESH
f32 = jnp.float32
bf16 = jnp.bfloat16


def dot(a, b, dims=((1,), (0,))):
    return lax.dot_general(a, b, (dims, ((), ())), preferred_element_type=f32)


NT = ((1,), (1,))
TN = ((0,), (0,))


def widen(cols):
    rows = cols.shape[0]
    return jnp.concatenate(
        [jnp.broadcast_to(cols[:, h : h + 1], (rows, HEAD_DIM)) for h in range(HEADS)], axis=1
    )


def one_minus_exp(w):
    series = 1.0 - w * (1.0 / 9.0)
    for k in (8, 7, 6, 5, 4, 3, 2):
        series = 1.0 - w * (1.0 / k) * series
    return jnp.where(w < 0.5, w * series, 1.0 - jnp.exp(-w))


def kernel(
    n, m, seq_len,
    x_hbm, b_hbm, c_hbm, dt_hbm, arow_ref, w_hbm, g_hbm,
    out_hbm, gin_hbm, gwrite_hbm, gread_hbm, gw_hbm,
    x_ref, b_ref, c_ref, dt_ref, w_ref, g_ref,
    out_ref, gin_ref, gwrite_ref, gread_ref, gw_ref,
    gsend, gall, gpsend, gprecv, fsend, frecv, fback, fin, asend, arecv, aback, ain, oall,
    part0, part1, part2, part3, ybuf0, ybuf1, ybuf2, ybuf3, rsbuf0, rsbuf1, rsbuf2, rsbuf3,
    tsend, trecv, both0, both1, gwall2, gwall3,
    g_ss, g_rs, gp_ss, gp_rs, f_ss, f_rs, a_ss, a_rs, fb_ss, fb_rs, ab_ss, ab_rs,
    o_ss, o_rs, y_ss, y_rs, r_ss, r_rs, t_ss, t_rs, b_ss, b_rs, w_ss, w_rs, in_sem, out_sem,
):
    parts, ybufs = (part0, part1, part2, part3), (ybuf0, ybuf1, ybuf2, ybuf3)
    rsbufs = (rsbuf0, rsbuf1, rsbuf2, rsbuf3)
    boths, gwalls = (both0, both1), (None, None, gwall2, gwall3)
    me = lax.axis_index("seq")
    dp = lax.axis_index("dp")
    tokens = x_ref.shape[1]
    pairs = n // 2
    z, y = me // 2, lax.rem(me, 2)
    loads = [
        pltpu.make_async_copy(src, dst, in_sem.at[i])
        for i, (src, dst) in enumerate(
            [(dt_hbm, dt_ref), (x_hbm, x_ref), (b_hbm, b_ref), (c_hbm, c_ref), (g_hbm, g_ref), (w_hbm, w_ref)]
        )
    ]
    for load in loads:
        load.start()
    stores = [
        pltpu.make_async_copy(src, dst, out_sem.at[i])
        for i, (src, dst) in enumerate(
            [(out_ref, out_hbm), (gin_ref, gin_hbm), (gwrite_ref, gwrite_hbm), (gread_ref, gread_hbm), (gw_ref, gw_hbm)]
        )
    ]
    rows = CHANNELS // n
    per_head = HEAD_DIM // rows
    cols = gsend.shape[2]
    wide = gprecv.shape[1]
    base = 2 * wide
    side = lax.rem(dp, 2)

    def seq_copy(src, dst, ss, rs, k, wait):
        to = lax.rem(me + k, n)
        source = lax.rem(me + n - k, n)
        return pltpu.make_async_remote_copy(
            src_ref=src.at[to],
            dst_ref=dst.at[source] if wait else dst.at[me],
            send_sem=ss.at[k],
            recv_sem=rs.at[k],
            device_id={"seq": to},
            device_id_type=MESH,
        )

    def seq_start(src, dst, ss, rs):
        def body(k, carry):
            seq_copy(src, dst, ss, rs, k, False).start()
            return carry

        lax.fori_loop(1, n, body, 0)

    def seq_wait(src, dst, ss, rs):
        def body(k, carry):
            seq_copy(src, dst, ss, rs, k, True).wait()
            return carry

        lax.fori_loop(1, n, body, 0)

    def dp_copy(src, dst, ss, rs, k, wait):
        to = lax.rem(dp + k, m)
        source = lax.rem(dp + m - k, m)
        return pltpu.make_async_remote_copy(
            src_ref=src.at[to],
            dst_ref=dst.at[source] if wait else dst.at[dp],
            send_sem=ss.at[k],
            recv_sem=rs.at[k],
            device_id={"dp": to},
            device_id_type=MESH,
        )

    bits = [1 << i for i in reversed(range(m.bit_length() - 1))]

    def dp_send(buf, ss, rs, off, bit):
        slot = jnp.bitwise_xor(dp, off)
        return pltpu.make_async_remote_copy(
            src_ref=buf.at[slot],
            dst_ref=buf.at[slot],
            send_sem=ss.at[off + bit],
            recv_sem=rs.at[off + bit],
            device_id={"dp": jnp.bitwise_xor(dp, bit)},
            device_id_type=MESH,
        )

    def dp_arrived(buf, ss, rs, off):
        slot = jnp.bitwise_xor(dp, off)
        bit = off & -off
        pltpu.make_async_remote_copy(
            src_ref=buf.at[slot],
            dst_ref=buf.at[slot],
            send_sem=ss.at[off],
            recv_sem=rs.at[off],
            device_id={"dp": jnp.bitwise_xor(dp, bit)},
            device_id_type=MESH,
        ).wait_recv()

    def dp_own(buf, ss, rs):
        for bit in bits:
            dp_send(buf, ss, rs, 0, bit).start()

    def dp_rest(buf, ss, rs, here=()):
        here = set(here)
        for bit in bits:
            for off in range(2 * bit, m, 2 * bit):
                if off not in here:
                    dp_arrived(buf, ss, rs, off)
                    here.add(off)
                dp_send(buf, ss, rs, off, bit).start()
        for off in range(1, m):
            if off not in here:
                dp_arrived(buf, ss, rs, off)

    def dp_sent(buf, ss, rs):
        for bit in bits:
            for off in range(0, m, 2 * bit):
                dp_send(buf, ss, rs, off, bit).wait_send()

    barrier = pltpu.get_barrier_semaphore()

    def greet_seq(k, carry):
        pl.semaphore_signal(
            barrier, inc=1, device_id={"seq": lax.rem(me + k, n)}, device_id_type=MESH
        )
        return carry

    def greet_dp(k, carry):
        pl.semaphore_signal(
            barrier, inc=1, device_id={"dp": lax.rem(dp + k, m)}, device_id_type=MESH
        )
        return carry

    lax.fori_loop(1, n, greet_seq, 0)
    lax.fori_loop(1, m, greet_dp, 0)

    loads[0].wait()
    dt = dt_ref[0]
    at_row = lax.broadcasted_iota(jnp.int32, (tokens, tokens), 0)
    at_col = lax.broadcasted_iota(jnp.int32, (tokens, tokens), 1)
    lower = at_row >= at_col
    low_mat = lower.astype(f32).astype(bf16)
    eye = (at_row == at_col).astype(f32).astype(bf16)
    digits = [
        part_of.astype(f32).astype(bf16) for part_of in (dt & 127, (dt >> 7) & 127, dt >> 14)
    ]

    def joined(pieces):
        whole = [p.astype(jnp.int32) for p in pieces]
        return whole[0] + whole[1] * 128 + whole[2] * 16384

    cum_row = joined([dot(d, low_mat, NT) for d in digits])
    cum_col = joined([dot(low_mat, d, NT) for d in digits])
    dt_col = joined([dot(eye, d, NT) for d in digits])
    rate_row = arow_ref[...] * (1.0 / (8.0 * seq_len))
    same = lax.broadcasted_iota(jnp.int32, (HEADS, HEADS), 0) == lax.broadcasted_iota(
        jnp.int32, (HEADS, HEADS), 1
    )
    rate_col = jnp.sum(jnp.where(same, rate_row, 0.0), axis=1, keepdims=True)
    weight = jnp.sqrt(one_minus_exp(2.0 * (rate_row * dt_col.astype(f32))))
    head = jnp.exp(-(rate_row * cum_col.astype(f32)))
    tail = jnp.exp(-(rate_row * (cum_col[tokens - 1 :, :] - cum_col).astype(f32)))
    totals = jnp.broadcast_to(
        jnp.exp(-(rate_col * cum_row[:, tokens - 1 :].astype(f32))), (HEADS, STATE)
    )
    weight_w, head_w, tail_w = widen(weight), widen(head), widen(tail)

    for load in loads[1:4]:
        load.wait()
    b = b_ref[0]
    c = c_ref[0]
    weighted = x_ref[0].astype(f32) * weight_w
    tailed = (weighted * tail_w).astype(bf16)
    weighted = weighted.astype(bf16)
    own = dot(tailed, b, TN)
    fsend[:, :rows, :] = own.reshape(n, rows, STATE)
    fsend[:, rows:, :] = jnp.broadcast_to(totals[None], (n, HEADS, STATE))

    pl.semaphore_wait(barrier, n - 1 + m - 1)
    seq_start(fsend, frecv, f_ss, f_rs)

    loads[4].wait()
    grad = g_ref[0]
    for d in range(m):
        gsend[d] = grad[:, base + d * cols : base + (d + 1) * cols].astype(f32)
    low_cols, high_cols = grad[:, :wide].astype(f32), grad[:, wide:base].astype(f32)
    gpsend[...] = jnp.where(side == 0, high_cols, low_cols)
    gp_own = jnp.where(side == 0, low_cols, high_cols).astype(bf16)

    def pair_copy(src, dst, ss, rs):
        return pltpu.make_async_remote_copy(
            src_ref=src,
            dst_ref=dst,
            send_sem=ss,
            recv_sem=rs,
            device_id={"dp": jnp.bitwise_xor(dp, 1)},
            device_id_type=MESH,
        )

    gp_copy = pair_copy(gpsend, gprecv, gp_ss.at[0], gp_rs.at[0])

    def g_start(k, carry):
        dp_copy(gsend, gall, g_ss, g_rs, k, False).start()
        return carry

    def g_wait(k, carry):
        dp_copy(gsend, gall, g_ss, g_rs, k, True).wait()
        return carry

    lax.fori_loop(1, m, g_start, 0)
    gp_copy.start()
    gall[dp] = gsend[dp]

    my_head = (me * rows) // HEAD_DIM
    frecv[me] = fsend[me]

    def scan_rows(buf, back, reverse):
        def body(step, state):
            s = n - 1 - step if reverse else step
            back[s] = state
            decay = buf[s, pl.ds(rows + my_head, 1), :]
            return decay * state + buf[s, :rows, :]

        lax.fori_loop(0, n, body, jnp.zeros((rows, STATE), f32))

    scores = dot(c, b, NT)
    y_parts, gx_parts = [], []

    masks, mixes = [], []
    for h in range(HEADS):
        gap = (cum_col[:, h : h + 1] - cum_row[h : h + 1, :]).astype(f32)
        mask = jnp.exp(jnp.where(lower, (-rate_row[:, h : h + 1]) * gap, -jnp.inf))
        mixed = (mask * scores).astype(bf16)
        masks.append(mask)
        mixes.append(mixed)
        y_parts.append(dot(mixed, weighted[:, h * HEAD_DIM : (h + 1) * HEAD_DIM]))

    def backward(heads, pair):
        for h in heads:
            span = slice(h * HEAD_DIM, (h + 1) * HEAD_DIM)
            gx_parts.append(dot(mixes[h], grad_y[:, span], TN))
            pair = pair + masks[h] * dot(grad_y[:, span], weighted[:, span], NT)
        return pair

    seq_wait(fsend, frecv, f_ss, f_rs)
    scan_rows(frecv, fback, False)
    seq_start(fback, fin, fb_ss, fb_rs)
    fin[me] = fback[me]

    loads[5].wait()
    grad_y = dot(grad, w_ref[...], NT).astype(bf16)
    grad_dec = (grad_y.astype(f32) * head_w).astype(bf16)
    own_adj = dot(grad_dec, c, TN)
    asend[:, :rows, :] = own_adj.reshape(n, rows, STATE)
    asend[:, rows:, :] = jnp.broadcast_to(totals[None], (n, HEADS, STATE))
    seq_start(asend, arecv, a_ss, a_rs)
    arecv[me] = asend[me]
    pair = backward(range(HEADS // 2), jnp.zeros((tokens, tokens), f32))
    y_intra = jnp.concatenate(y_parts, axis=1)
    seq_wait(fback, fin, fb_ss, fb_rs)
    state_in = fin[...].reshape(CHANNELS, STATE).astype(bf16)
    out = (y_intra + dot(c, state_in, NT) * head_w).astype(bf16)
    halves = CHANNELS // HALF
    for j in range(halves):
        oall[j, dp] = out[:, j * HALF : (j + 1) * HALF].astype(f32)
        dp_own(oall.at[j], o_ss.at[j], o_rs.at[j])
    out_ref[0] = out
    stores[0].start()

    def to_partner(i):
        return pltpu.make_async_remote_copy(
            src_ref=parts[i].at[1 - y],
            dst_ref=ybufs[i],
            send_sem=y_ss.at[i],
            recv_sem=y_rs.at[i],
            device_id={"seq": 2 * z + 1 - y},
            device_id_type=MESH,
        )

    def to_owner(i, p, source):
        return pltpu.make_async_remote_copy(
            src_ref=parts[i].at[y, p],
            dst_ref=rsbufs[i].at[source],
            send_sem=r_ss.at[i, p],
            recv_sem=r_rs.at[i, source],
            device_id={"seq": 2 * p + y},
            device_id_type=MESH,
        )

    def send_part(i, total):
        split = total.reshape(pairs, 2, rows, total.shape[1])
        parts[i][0] = split[:, 0]
        parts[i][1] = split[:, 1]
        to_partner(i).start()

    def join(i):
        to_partner(i).wait_recv()
        parts[i][y] = parts[i][y] + ybufs[i][...]

        def body(k, carry):
            to_owner(i, lax.rem(z + k, pairs), z).start()
            return carry

        lax.fori_loop(1, pairs, body, 0)

    def owned(i):
        def body(k, acc):
            source = lax.rem(z + k, pairs)
            to_owner(i, source, source).wait()
            return acc + rsbufs[i][source]

        return lax.fori_loop(1, pairs, body, parts[i][y, z])

    gp_copy.wait()
    gp_got = gprecv[...].astype(bf16)
    mate = jnp.bitwise_xor(dp, 1)
    for j in range(halves):
        dp_arrived(oall.at[j], o_ss.at[j], o_rs.at[j], 1)
    mate_out = [oall[j, mate].astype(bf16) for j in range(halves)]
    for i, (paired, start, size) in enumerate(PIECES):
        if paired:
            at = slice(start, start + size)
            own_sum = dot(out, gp_own[:, at], TN)
            mate_sum = jnp.concatenate([dot(o, gp_got[:, at], TN) for o in mate_out], axis=0)
            send_part(i, own_sum + mate_sum)
    seq_wait(asend, arecv, a_ss, a_rs)
    scan_rows(arecv, aback, True)
    seq_start(aback, ain, ab_ss, ab_rs)
    ain[me] = aback[me]
    pair = backward(range(HEADS // 2, HEADS), pair)
    gx_intra = jnp.concatenate(gx_parts, axis=1)
    pair = pair.astype(bf16)
    read_intra = dot(pair, b)
    write_intra = dot(pair, c, TN)
    gread_ref[0] = (read_intra + dot(grad_dec, state_in)).astype(bf16)
    stores[3].start()
    lax.fori_loop(1, m, g_wait, 0)
    gall_half = [gall[d].astype(bf16) for d in range(m)]
    for i in range(2):
        join(i)
        dp_rest(oall.at[i], o_ss.at[i], o_rs.at[i], (1,))

    for i, (paired, start, size) in enumerate(PIECES):
        if not paired:
            at = slice(start, start + size)
            blocks = []
            for j in range(halves):
                total = jnp.zeros((HALF, size), f32)
                for d in range(m):
                    total = total + dot(oall[j, d].astype(bf16), gall_half[d][:, at], TN)
                blocks.append(total)
            send_part(i, jnp.concatenate(blocks, axis=0))

    seq_wait(aback, ain, ab_ss, ab_rs)
    adj_in = ain[...].reshape(CHANNELS, STATE).astype(bf16)
    gwrite_ref[0] = (write_intra + dot(tailed, adj_in)).astype(bf16)
    stores[2].start()
    gin_ref[0] = ((gx_intra + tail_w * dot(b, adj_in, NT)) * weight_w).astype(bf16)
    stores[1].start()

    def across(i, at):
        return pltpu.make_async_remote_copy(
            src_ref=tsend.at[i, at],
            dst_ref=trecv.at[i, at],
            send_sem=t_ss.at[i, at],
            recv_sem=t_rs.at[i, at],
            device_id={"dp": jnp.bitwise_xor(dp, bits[at])},
            device_id_type=MESH,
        )

    far = len(bits) - 1
    for i in range(2):
        tsend[i, 0] = owned(i)
        across(i, 0).start()
        join(2 + i)

    def finish_pair(i):
        for at in range(far):
            across(i, at).wait()
            total = tsend[i, at] + trecv[i, at]
            if at + 1 < far:
                tsend[i, at + 1] = total
                across(i, at + 1).start()
        boths[i][side] = total
        pair_copy(boths[i].at[side], boths[i].at[side], b_ss.at[i], b_rs.at[i]).start()

    for i in range(2):
        finish_pair(i)
    for i in (2, 3):
        gwalls[i][dp] = owned(i)
        dp_own(gwalls[i], w_ss.at[i - 2], w_rs.at[i - 2])

    for i in range(2):
        pair_copy(boths[i].at[side], boths[i].at[1 - side], b_ss.at[i], b_rs.at[i]).wait()
        start, size = PIECES[i][1:]
        for d in range(2):
            gw_ref[:, d * wide + start : d * wide + start + size] = boths[i][d]
    for i in (2, 3):
        dp_rest(gwalls[i], w_ss.at[i - 2], w_rs.at[i - 2])
        start, size = PIECES[i][1:]
        for d in range(m):
            at = base + d * cols + start
            gw_ref[:, at : at + size] = gwalls[i][d]
    stores[4].start()

    for i in range(len(PIECES)):
        to_partner(i).wait_send()
    for j in range(halves):
        dp_sent(oall.at[j], o_ss.at[j], o_rs.at[j])
    for i in range(2):
        dp_sent(gwalls[2 + i], w_ss.at[i], w_rs.at[i])
    for store in stores:
        store.wait()


def settle(*refs):
    sources, results, held = refs[:5], refs[5:10], refs[10:15]
    in_sem, out_sem = refs[15:]
    loads = [pltpu.make_async_copy(sources[i], held[i], in_sem.at[i]) for i in range(5)]
    stores = [pltpu.make_async_copy(held[i], results[i], out_sem.at[i]) for i in range(5)]
    for load in loads:
        load.start()
    for load, store in zip(loads, stores):
        load.wait()
        store.start()
    for store in stores:
        store.wait()


def solution(mesh):
    n, m = mesh.shape["seq"], mesh.shape["dp"]

    def shards(inputs, write_vecs, read_vecs, dt_code, a_rate, w_out, grad_out):
        tokens, width = inputs.shape[1], grad_out.shape[2]
        rows, cols = CHANNELS // n, ALONE
        paired_cols = (width - m * ALONE) // 2
        far = m.bit_length() - 2
        hbm = pl.BlockSpec(memory_space=pltpu.MemorySpace.HBM)
        vm = pl.BlockSpec(memory_space=pltpu.VMEM)
        sems = []
        for shape in ((m,), (1,), (n,), (n,), (n,), (n,), (2, m), (4,), (4, n // 2), (2, far), (2,), (2, m)):
            sems += [pltpu.SemaphoreType.DMA(shape)] * 2
        wide, plain = (n, rows + HEADS, STATE), (n, rows, STATE)
        results = (
            jax.ShapeDtypeStruct((1, tokens, CHANNELS), bf16),
            jax.ShapeDtypeStruct((1, tokens, CHANNELS), bf16),
            jax.ShapeDtypeStruct((1, tokens, STATE), bf16),
            jax.ShapeDtypeStruct((1, tokens, STATE), bf16),
            jax.ShapeDtypeStruct((rows, width), f32),
        )
        args = (inputs, write_vecs, read_vecs, dt_code, w_out, grad_out)
        held = pl.pallas_call(
            functools.partial(kernel, n, m, float(tokens * n)),
            out_shape=results,
            in_specs=[hbm] * 4 + [vm] + [hbm] * 2,
            out_specs=(hbm,) * 5,
            scratch_shapes=[pltpu.VMEM(a.shape, a.dtype) for a in args]
            + [pltpu.VMEM(a.shape, a.dtype) for a in results]
            + [
                pltpu.VMEM((m, tokens, cols), f32),
                pltpu.VMEM((m, tokens, cols), f32),
                pltpu.VMEM((tokens, paired_cols), f32),
                pltpu.VMEM((tokens, paired_cols), f32),
                pltpu.VMEM(wide, f32),
                pltpu.VMEM(wide, f32),
                pltpu.VMEM(plain, f32),
                pltpu.VMEM(plain, f32),
                pltpu.VMEM(wide, f32),
                pltpu.VMEM(wide, f32),
                pltpu.VMEM(plain, f32),
                pltpu.VMEM(plain, f32),
                pltpu.VMEM((2, m, tokens, HALF), f32),
            ]
            + [pltpu.VMEM((2, n // 2, rows, size), f32) for _, _, size in PIECES]
            + [pltpu.VMEM((n // 2, rows, size), f32) for _, _, size in PIECES] * 2
            + [pltpu.VMEM((2, far, rows, PIECES[0][2]), f32)] * 2
            + [pltpu.VMEM((2, rows, size), f32) for _, _, size in PIECES[:2]]
            + [pltpu.VMEM((m, rows, size), f32) for _, _, size in PIECES[2:]]
            + sems
            + [pltpu.SemaphoreType.DMA((6,)), pltpu.SemaphoreType.DMA((5,))],
            compiler_params=pltpu.CompilerParams(
                collective_id=0, has_side_effects=True, vmem_limit_bytes=VMEM_BYTES
            ),
            name="scan_core",
        )(inputs, write_vecs, read_vecs, dt_code, a_rate.reshape(1, HEADS), w_out, grad_out)
        return pl.pallas_call(
            settle,
            out_shape=results,
            in_specs=[hbm] * 5,
            out_specs=(hbm,) * 5,
            scratch_shapes=[pltpu.VMEM(a.shape, a.dtype) for a in results]
            + [pltpu.SemaphoreType.DMA((5,)), pltpu.SemaphoreType.DMA((5,))],
            compiler_params=pltpu.CompilerParams(vmem_limit_bytes=VMEM_BYTES),
            name="settle",
        )(*held)

    placed = (
        P("dp", "seq", None),
        P("dp", "seq", None),
        P("dp", "seq", None),
        P("dp", None, "seq"),
        P(),
        P(),
        P("dp", "seq", None),
    )
    return jax.shard_map(
        shards,
        mesh=mesh,
        in_specs=placed,
        out_specs=(
            P("dp", "seq", None),
            P("dp", "seq", None),
            P("dp", "seq", None),
            P("dp", "seq", None),
            P("seq", None),
        ),
        check_vma=False,
    )
```

```python
import functools

import jax
import jax.numpy as jnp
from jax import lax
from jax.experimental import pallas as pl
from jax.experimental.pallas import tpu as pltpu
from jax.sharding import PartitionSpec as P

HEAD_DIM = 64
STATE = 128
HEADS = 8
HALF = 256
ALONE = 384
PIECES = ((True, 0, 256), (True, 256, 256), (False, 0, 256), (False, 256, 128))
VMEM_BYTES = 60 * 1024 * 1024
CHANNELS = HEADS * HEAD_DIM
MESH = pl.DeviceIdType.MESH
f32 = jnp.float32
bf16 = jnp.bfloat16


def dot(a, b, dims=((1,), (0,))):
    return lax.dot_general(a, b, (dims, ((), ())), preferred_element_type=f32)


NT = ((1,), (1,))
TN = ((0,), (0,))


def widen(cols):
    rows = cols.shape[0]
    return jnp.concatenate(
        [jnp.broadcast_to(cols[:, h : h + 1], (rows, HEAD_DIM)) for h in range(HEADS)], axis=1
    )


def one_minus_exp(w):
    series = 1.0 - w * (1.0 / 9.0)
    for k in (8, 7, 6, 5, 4, 3, 2):
        series = 1.0 - w * (1.0 / k) * series
    return jnp.where(w < 0.5, w * series, 1.0 - jnp.exp(-w))


def kernel(
    n, m, seq_len,
    x_hbm, b_hbm, c_hbm, dt_hbm, arow_ref, w_hbm, g_hbm,
    out_hbm, gin_hbm, gwrite_hbm, gread_hbm, gw_hbm,
    x_ref, b_ref, c_ref, dt_ref, w_ref, g_ref,
    out_ref, gin_ref, gwrite_ref, gread_ref, gw_ref,
    gsend, gall, gpsend, gprecv, fsend, frecv, fback, fin, asend, arecv, aback, ain, oall,
    part0, part1, part2, part3, ybuf0, ybuf1, ybuf2, ybuf3, rsbuf0, rsbuf1, rsbuf2, rsbuf3,
    tsend, trecv, both0, both1, gwall2, gwall3,
    g_ss, g_rs, gp_ss, gp_rs, f_ss, f_rs, a_ss, a_rs, fb_ss, fb_rs, ab_ss, ab_rs,
    o_ss, o_rs, y_ss, y_rs, r_ss, r_rs, t_ss, t_rs, b_ss, b_rs, w_ss, w_rs, in_sem, out_sem,
):
    parts, ybufs = (part0, part1, part2, part3), (ybuf0, ybuf1, ybuf2, ybuf3)
    rsbufs = (rsbuf0, rsbuf1, rsbuf2, rsbuf3)
    boths, gwalls = (both0, both1), (None, None, gwall2, gwall3)
    me = lax.axis_index("seq")
    dp = lax.axis_index("dp")
    tokens = x_ref.shape[1]
    pairs = n // 2
    z, y = me // 2, lax.rem(me, 2)
    loads = [
        pltpu.make_async_copy(src, dst, in_sem.at[i])
        for i, (src, dst) in enumerate(
            [(dt_hbm, dt_ref), (x_hbm, x_ref), (b_hbm, b_ref), (c_hbm, c_ref), (g_hbm, g_ref), (w_hbm, w_ref)]
        )
    ]
    for load in loads:
        load.start()
    stores = [
        pltpu.make_async_copy(src, dst, out_sem.at[i])
        for i, (src, dst) in enumerate(
            [(out_ref, out_hbm), (gin_ref, gin_hbm), (gwrite_ref, gwrite_hbm), (gread_ref, gread_hbm), (gw_ref, gw_hbm)]
        )
    ]
    rows = CHANNELS // n
    per_head = HEAD_DIM // rows
    cols = gsend.shape[2]
    wide = gprecv.shape[1]
    base = 2 * wide
    side = lax.rem(dp, 2)

    def seq_copy(src, dst, ss, rs, k, wait):
        to = lax.rem(me + k, n)
        source = lax.rem(me + n - k, n)
        return pltpu.make_async_remote_copy(
            src_ref=src.at[to],
            dst_ref=dst.at[source] if wait else dst.at[me],
            send_sem=ss.at[k],
            recv_sem=rs.at[k],
            device_id={"seq": to},
            device_id_type=MESH,
        )

    def seq_start(src, dst, ss, rs):
        def body(k, carry):
            seq_copy(src, dst, ss, rs, k, False).start()
            return carry

        lax.fori_loop(1, n, body, 0)

    def seq_wait(src, dst, ss, rs):
        def body(k, carry):
            seq_copy(src, dst, ss, rs, k, True).wait()
            return carry

        lax.fori_loop(1, n, body, 0)

    def dp_copy(src, dst, ss, rs, k, wait):
        to = lax.rem(dp + k, m)
        source = lax.rem(dp + m - k, m)
        return pltpu.make_async_remote_copy(
            src_ref=src.at[to],
            dst_ref=dst.at[source] if wait else dst.at[dp],
            send_sem=ss.at[k],
            recv_sem=rs.at[k],
            device_id={"dp": to},
            device_id_type=MESH,
        )

    bits = [1 << i for i in reversed(range(m.bit_length() - 1))]

    def dp_send(buf, ss, rs, off, bit):
        slot = jnp.bitwise_xor(dp, off)
        return pltpu.make_async_remote_copy(
            src_ref=buf.at[slot],
            dst_ref=buf.at[slot],
            send_sem=ss.at[off + bit],
            recv_sem=rs.at[off + bit],
            device_id={"dp": jnp.bitwise_xor(dp, bit)},
            device_id_type=MESH,
        )

    def dp_arrived(buf, ss, rs, off):
        slot = jnp.bitwise_xor(dp, off)
        bit = off & -off
        pltpu.make_async_remote_copy(
            src_ref=buf.at[slot],
            dst_ref=buf.at[slot],
            send_sem=ss.at[off],
            recv_sem=rs.at[off],
            device_id={"dp": jnp.bitwise_xor(dp, bit)},
            device_id_type=MESH,
        ).wait_recv()

    def dp_own(buf, ss, rs):
        for bit in bits:
            dp_send(buf, ss, rs, 0, bit).start()

    def dp_rest(buf, ss, rs, here=()):
        here = set(here)
        for bit in bits:
            for off in range(2 * bit, m, 2 * bit):
                if off not in here:
                    dp_arrived(buf, ss, rs, off)
                    here.add(off)
                dp_send(buf, ss, rs, off, bit).start()
        for off in range(1, m):
            if off not in here:
                dp_arrived(buf, ss, rs, off)

    def dp_sent(buf, ss, rs):
        for bit in bits:
            for off in range(0, m, 2 * bit):
                dp_send(buf, ss, rs, off, bit).wait_send()

    barrier = pltpu.get_barrier_semaphore()

    def greet_seq(k, carry):
        pl.semaphore_signal(
            barrier, inc=1, device_id={"seq": lax.rem(me + k, n)}, device_id_type=MESH
        )
        return carry

    def greet_dp(k, carry):
        pl.semaphore_signal(
            barrier, inc=1, device_id={"dp": lax.rem(dp + k, m)}, device_id_type=MESH
        )
        return carry

    lax.fori_loop(1, n, greet_seq, 0)
    lax.fori_loop(1, m, greet_dp, 0)

    loads[0].wait()
    dt = dt_ref[0]
    at_row = lax.broadcasted_iota(jnp.int32, (tokens, tokens), 0)
    at_col = lax.broadcasted_iota(jnp.int32, (tokens, tokens), 1)
    lower = at_row >= at_col
    low_mat = lower.astype(f32).astype(bf16)
    eye = (at_row == at_col).astype(f32).astype(bf16)
    digits = [
        part_of.astype(f32).astype(bf16) for part_of in (dt & 127, (dt >> 7) & 127, dt >> 14)
    ]

    def joined(pieces):
        whole = [p.astype(jnp.int32) for p in pieces]
        return whole[0] + whole[1] * 128 + whole[2] * 16384

    cum_row = joined([dot(d, low_mat, NT) for d in digits])
    cum_col = joined([dot(low_mat, d, NT) for d in digits])
    dt_col = joined([dot(eye, d, NT) for d in digits])
    rate_row = arow_ref[...] * (1.0 / (8.0 * seq_len))
    same = lax.broadcasted_iota(jnp.int32, (HEADS, HEADS), 0) == lax.broadcasted_iota(
        jnp.int32, (HEADS, HEADS), 1
    )
    rate_col = jnp.sum(jnp.where(same, rate_row, 0.0), axis=1, keepdims=True)
    weight = jnp.sqrt(one_minus_exp(2.0 * (rate_row * dt_col.astype(f32))))
    head = jnp.exp(-(rate_row * cum_col.astype(f32)))
    tail = jnp.exp(-(rate_row * (cum_col[tokens - 1 :, :] - cum_col).astype(f32)))
    totals = jnp.broadcast_to(
        jnp.exp(-(rate_col * cum_row[:, tokens - 1 :].astype(f32))), (HEADS, STATE)
    )
    weight_w, head_w, tail_w = widen(weight), widen(head), widen(tail)

    for load in loads[1:4]:
        load.wait()
    b = b_ref[0]
    c = c_ref[0]
    weighted = x_ref[0].astype(f32) * weight_w
    tailed = (weighted * tail_w).astype(bf16)
    weighted = weighted.astype(bf16)
    own = dot(tailed, b, TN)
    fsend[:, :rows, :] = own.reshape(n, rows, STATE)
    fsend[:, rows:, :] = jnp.broadcast_to(totals[None], (n, HEADS, STATE))

    pl.semaphore_wait(barrier, n - 1 + m - 1)
    seq_start(fsend, frecv, f_ss, f_rs)

    loads[4].wait()
    grad = g_ref[0]
    for d in range(m):
        gsend[d] = grad[:, base + d * cols : base + (d + 1) * cols].astype(f32)
    low_cols, high_cols = grad[:, :wide].astype(f32), grad[:, wide:base].astype(f32)
    gpsend[...] = jnp.where(side == 0, high_cols, low_cols)
    gp_own = jnp.where(side == 0, low_cols, high_cols).astype(bf16)

    def pair_copy(src, dst, ss, rs):
        return pltpu.make_async_remote_copy(
            src_ref=src,
            dst_ref=dst,
            send_sem=ss,
            recv_sem=rs,
            device_id={"dp": jnp.bitwise_xor(dp, 1)},
            device_id_type=MESH,
        )

    gp_copy = pair_copy(gpsend, gprecv, gp_ss.at[0], gp_rs.at[0])

    def g_start(k, carry):
        dp_copy(gsend, gall, g_ss, g_rs, k, False).start()
        return carry

    def g_wait(k, carry):
        dp_copy(gsend, gall, g_ss, g_rs, k, True).wait()
        return carry

    lax.fori_loop(1, m, g_start, 0)
    gp_copy.start()
    gall[dp] = gsend[dp]

    my_head = (me * rows) // HEAD_DIM
    frecv[me] = fsend[me]

    def scan_rows(buf, back, reverse):
        def body(step, state):
            s = n - 1 - step if reverse else step
            back[s] = state
            decay = buf[s, pl.ds(rows + my_head, 1), :]
            return decay * state + buf[s, :rows, :]

        lax.fori_loop(0, n, body, jnp.zeros((rows, STATE), f32))

    scores = dot(c, b, NT)
    y_parts, gx_parts = [], []

    masks, mixes = [], []
    for h in range(HEADS):
        gap = (cum_col[:, h : h + 1] - cum_row[h : h + 1, :]).astype(f32)
        mask = jnp.exp(jnp.where(lower, (-rate_row[:, h : h + 1]) * gap, -jnp.inf))
        mixed = (mask * scores).astype(bf16)
        masks.append(mask)
        mixes.append(mixed)
        y_parts.append(dot(mixed, weighted[:, h * HEAD_DIM : (h + 1) * HEAD_DIM]))

    def backward(heads, pair):
        for h in heads:
            span = slice(h * HEAD_DIM, (h + 1) * HEAD_DIM)
            gx_parts.append(dot(mixes[h], grad_y[:, span], TN))
            pair = pair + masks[h] * dot(grad_y[:, span], weighted[:, span], NT)
        return pair

    seq_wait(fsend, frecv, f_ss, f_rs)
    scan_rows(frecv, fback, False)
    seq_start(fback, fin, fb_ss, fb_rs)
    fin[me] = fback[me]

    loads[5].wait()
    grad_y = dot(grad, w_ref[...], NT).astype(bf16)
    grad_dec = (grad_y.astype(f32) * head_w).astype(bf16)
    own_adj = dot(grad_dec, c, TN)
    asend[:, :rows, :] = own_adj.reshape(n, rows, STATE)
    asend[:, rows:, :] = jnp.broadcast_to(totals[None], (n, HEADS, STATE))
    seq_start(asend, arecv, a_ss, a_rs)
    arecv[me] = asend[me]
    pair = backward(range(HEADS // 2), jnp.zeros((tokens, tokens), f32))
    y_intra = jnp.concatenate(y_parts, axis=1)
    seq_wait(fback, fin, fb_ss, fb_rs)
    state_in = fin[...].reshape(CHANNELS, STATE).astype(bf16)
    out = (y_intra + dot(c, state_in, NT) * head_w).astype(bf16)
    halves = CHANNELS // HALF
    for j in range(halves):
        oall[j, dp] = out[:, j * HALF : (j + 1) * HALF].astype(f32)
        dp_own(oall.at[j], o_ss.at[j], o_rs.at[j])
    out_ref[0] = out
    stores[0].start()

    def to_partner(i):
        return pltpu.make_async_remote_copy(
            src_ref=parts[i].at[1 - y],
            dst_ref=ybufs[i],
            send_sem=y_ss.at[i],
            recv_sem=y_rs.at[i],
            device_id={"seq": 2 * z + 1 - y},
            device_id_type=MESH,
        )

    def to_owner(i, p, source):
        return pltpu.make_async_remote_copy(
            src_ref=parts[i].at[y, p],
            dst_ref=rsbufs[i].at[source],
            send_sem=r_ss.at[i, p],
            recv_sem=r_rs.at[i, source],
            device_id={"seq": 2 * p + y},
            device_id_type=MESH,
        )

    def send_part(i, total):
        split = total.reshape(pairs, 2, rows, total.shape[1])
        parts[i][0] = split[:, 0]
        parts[i][1] = split[:, 1]
        to_partner(i).start()

    def join(i):
        to_partner(i).wait_recv()
        parts[i][y] = parts[i][y] + ybufs[i][...]

        def body(k, carry):
            to_owner(i, lax.rem(z + k, pairs), z).start()
            return carry

        lax.fori_loop(1, pairs, body, 0)

    def owned(i):
        def body(k, acc):
            source = lax.rem(z + k, pairs)
            to_owner(i, source, source).wait()
            return acc + rsbufs[i][source]

        return lax.fori_loop(1, pairs, body, parts[i][y, z])

    gp_copy.wait()
    gp_got = gprecv[...].astype(bf16)
    mate = jnp.bitwise_xor(dp, 1)
    for j in range(halves):
        dp_arrived(oall.at[j], o_ss.at[j], o_rs.at[j], 1)
    mate_out = [oall[j, mate].astype(bf16) for j in range(halves)]
    for i, (paired, start, size) in enumerate(PIECES):
        if paired:
            at = slice(start, start + size)
            own_sum = dot(out, gp_own[:, at], TN)
            mate_sum = jnp.concatenate([dot(o, gp_got[:, at], TN) for o in mate_out], axis=0)
            send_part(i, own_sum + mate_sum)
    seq_wait(asend, arecv, a_ss, a_rs)
    scan_rows(arecv, aback, True)
    seq_start(aback, ain, ab_ss, ab_rs)
    ain[me] = aback[me]
    lax.fori_loop(1, m, g_wait, 0)
    gall_half = [gall[d].astype(bf16) for d in range(m)]
    join(0)
    dp_rest(oall.at[0], o_ss.at[0], o_rs.at[0], (1,))
    pair = backward(range(HEADS // 2, HEADS), pair)
    gx_intra = jnp.concatenate(gx_parts, axis=1)
    pair = pair.astype(bf16)
    read_intra = dot(pair, b)
    write_intra = dot(pair, c, TN)
    gread_ref[0] = (read_intra + dot(grad_dec, state_in)).astype(bf16)
    stores[3].start()
    join(1)
    dp_rest(oall.at[1], o_ss.at[1], o_rs.at[1], (1,))

    for i, (paired, start, size) in enumerate(PIECES):
        if not paired:
            at = slice(start, start + size)
            blocks = []
            for j in range(halves):
                total = jnp.zeros((HALF, size), f32)
                for d in range(m):
                    total = total + dot(oall[j, d].astype(bf16), gall_half[d][:, at], TN)
                blocks.append(total)
            send_part(i, jnp.concatenate(blocks, axis=0))

    seq_wait(aback, ain, ab_ss, ab_rs)
    adj_in = ain[...].reshape(CHANNELS, STATE).astype(bf16)
    gwrite_ref[0] = (write_intra + dot(tailed, adj_in)).astype(bf16)
    stores[2].start()
    gin_ref[0] = ((gx_intra + tail_w * dot(b, adj_in, NT)) * weight_w).astype(bf16)
    stores[1].start()

    def across(i, at):
        return pltpu.make_async_remote_copy(
            src_ref=tsend.at[i, at],
            dst_ref=trecv.at[i, at],
            send_sem=t_ss.at[i, at],
            recv_sem=t_rs.at[i, at],
            device_id={"dp": jnp.bitwise_xor(dp, bits[at])},
            device_id_type=MESH,
        )

    far = len(bits) - 1
    for i in range(2):
        tsend[i, 0] = owned(i)
        across(i, 0).start()
        join(2 + i)

    def finish_pair(i):
        for at in range(far):
            across(i, at).wait()
            total = tsend[i, at] + trecv[i, at]
            if at + 1 < far:
                tsend[i, at + 1] = total
                across(i, at + 1).start()
        boths[i][side] = total
        pair_copy(boths[i].at[side], boths[i].at[side], b_ss.at[i], b_rs.at[i]).start()

    for i in range(2):
        finish_pair(i)
    for i in (2, 3):
        gwalls[i][dp] = owned(i)
        dp_own(gwalls[i], w_ss.at[i - 2], w_rs.at[i - 2])

    for i in range(2):
        pair_copy(boths[i].at[side], boths[i].at[1 - side], b_ss.at[i], b_rs.at[i]).wait()
        start, size = PIECES[i][1:]
        for d in range(2):
            gw_ref[:, d * wide + start : d * wide + start + size] = boths[i][d]
    for i in (2, 3):
        dp_rest(gwalls[i], w_ss.at[i - 2], w_rs.at[i - 2])
        start, size = PIECES[i][1:]
        for d in range(m):
            at = base + d * cols + start
            gw_ref[:, at : at + size] = gwalls[i][d]
    stores[4].start()

    for i in range(len(PIECES)):
        to_partner(i).wait_send()
    for j in range(halves):
        dp_sent(oall.at[j], o_ss.at[j], o_rs.at[j])
    for i in range(2):
        dp_sent(gwalls[2 + i], w_ss.at[i], w_rs.at[i])
    for store in stores:
        store.wait()


def settle(*refs):
    sources, results, held = refs[:5], refs[5:10], refs[10:15]
    in_sem, out_sem = refs[15:]
    loads = [pltpu.make_async_copy(sources[i], held[i], in_sem.at[i]) for i in range(5)]
    stores = [pltpu.make_async_copy(held[i], results[i], out_sem.at[i]) for i in range(5)]
    for load in loads:
        load.start()
    for load, store in zip(loads, stores):
        load.wait()
        store.start()
    for store in stores:
        store.wait()


def solution(mesh):
    n, m = mesh.shape["seq"], mesh.shape["dp"]

    def shards(inputs, write_vecs, read_vecs, dt_code, a_rate, w_out, grad_out):
        tokens, width = inputs.shape[1], grad_out.shape[2]
        rows, cols = CHANNELS // n, ALONE
        paired_cols = (width - m * ALONE) // 2
        far = m.bit_length() - 2
        hbm = pl.BlockSpec(memory_space=pltpu.MemorySpace.HBM)
        vm = pl.BlockSpec(memory_space=pltpu.VMEM)
        sems = []
        for shape in ((m,), (1,), (n,), (n,), (n,), (n,), (2, m), (4,), (4, n // 2), (2, far), (2,), (2, m)):
            sems += [pltpu.SemaphoreType.DMA(shape)] * 2
        wide, plain = (n, rows + HEADS, STATE), (n, rows, STATE)
        results = (
            jax.ShapeDtypeStruct((1, tokens, CHANNELS), bf16),
            jax.ShapeDtypeStruct((1, tokens, CHANNELS), bf16),
            jax.ShapeDtypeStruct((1, tokens, STATE), bf16),
            jax.ShapeDtypeStruct((1, tokens, STATE), bf16),
            jax.ShapeDtypeStruct((rows, width), f32),
        )
        args = (inputs, write_vecs, read_vecs, dt_code, w_out, grad_out)
        held = pl.pallas_call(
            functools.partial(kernel, n, m, float(tokens * n)),
            out_shape=results,
            in_specs=[hbm] * 4 + [vm] + [hbm] * 2,
            out_specs=(hbm,) * 5,
            scratch_shapes=[pltpu.VMEM(a.shape, a.dtype) for a in args]
            + [pltpu.VMEM(a.shape, a.dtype) for a in results]
            + [
                pltpu.VMEM((m, tokens, cols), f32),
                pltpu.VMEM((m, tokens, cols), f32),
                pltpu.VMEM((tokens, paired_cols), f32),
                pltpu.VMEM((tokens, paired_cols), f32),
                pltpu.VMEM(wide, f32),
                pltpu.VMEM(wide, f32),
                pltpu.VMEM(plain, f32),
                pltpu.VMEM(plain, f32),
                pltpu.VMEM(wide, f32),
                pltpu.VMEM(wide, f32),
                pltpu.VMEM(plain, f32),
                pltpu.VMEM(plain, f32),
                pltpu.VMEM((2, m, tokens, HALF), f32),
            ]
            + [pltpu.VMEM((2, n // 2, rows, size), f32) for _, _, size in PIECES]
            + [pltpu.VMEM((n // 2, rows, size), f32) for _, _, size in PIECES] * 2
            + [pltpu.VMEM((2, far, rows, PIECES[0][2]), f32)] * 2
            + [pltpu.VMEM((2, rows, size), f32) for _, _, size in PIECES[:2]]
            + [pltpu.VMEM((m, rows, size), f32) for _, _, size in PIECES[2:]]
            + sems
            + [pltpu.SemaphoreType.DMA((6,)), pltpu.SemaphoreType.DMA((5,))],
            compiler_params=pltpu.CompilerParams(
                collective_id=0, has_side_effects=True, vmem_limit_bytes=VMEM_BYTES
            ),
            name="scan_core",
        )(inputs, write_vecs, read_vecs, dt_code, a_rate.reshape(1, HEADS), w_out, grad_out)
        return pl.pallas_call(
            settle,
            out_shape=results,
            in_specs=[hbm] * 5,
            out_specs=(hbm,) * 5,
            scratch_shapes=[pltpu.VMEM(a.shape, a.dtype) for a in results]
            + [pltpu.SemaphoreType.DMA((5,)), pltpu.SemaphoreType.DMA((5,))],
            compiler_params=pltpu.CompilerParams(vmem_limit_bytes=VMEM_BYTES),
            name="settle",
        )(*held)

    placed = (
        P("dp", "seq", None),
        P("dp", "seq", None),
        P("dp", "seq", None),
        P("dp", None, "seq"),
        P(),
        P(),
        P("dp", "seq", None),
    )
    return jax.shard_map(
        shards,
        mesh=mesh,
        in_specs=placed,
        out_specs=(
            P("dp", "seq", None),
            P("dp", "seq", None),
            P("dp", "seq", None),
            P("dp", "seq", None),
            P("seq", None),
        ),
        check_vma=False,
    )
```
